256 devices in a mesh: dp: 32 (over y, x, core), ulysses: 8 (over z).
Axes of the slice: x: 4, y: 4, z: 8, core: 2. Of those that a mesh axis runs over, the one named last changes fastest.
Arguments:
- query_in: bfloat16 [65536, 3072], P(('dp', 'ulysses')), may hold values from -6 to 6
- key_in: bfloat16 [65536, 3072], P(('dp', 'ulysses')), may hold values from -6 to 6
- value_in: bfloat16 [65536, 3072], P(('dp', 'ulysses')), may hold values from -6 to 6
- grad_out: bfloat16 [65536, 3072], P('dp', 'ulysses'), may hold values from -6 to 6
- packing: int32 [512], replicated, may hold values from 0 to 511, as said below
- doc_tiles: int32 [32, 5], P('dp'), may hold values from 1 to 4, 16 in all within a row
Outputs:
- attended: bfloat16 [65536, 3072], P('dp', 'ulysses')
- grad_query: bfloat16 [65536, 3072], P(('dp', 'ulysses'))
- grad_key: bfloat16 [65536, 3072], P(('dp', 'ulysses'))
- grad_value: bfloat16 [65536, 3072], P(('dp', 'ulysses'))
The draws below stay inside these ranges and needn't reach their ends.
Inputs may be any that keep to these rules, and one draw needn't show every extreme that they name: packing fills every packed tile exactly once; tile g goes to packed row packing[g] // 16, slot packing[g] % 16; from the 16 tiles of one delivered row at most 1 go to one packed row, and that many do for some pairs of rows in every draw. Each row of doc_tiles sums to 16, and in each row some document has 4 tiles.
All inputs are finite; a program needn't handle non-finite values.
Results may differ from the reference program's by a relative error of at most 0.028.
Values may be sent and summed in bfloat16 or wider, within the bound.
No kernel may reach another device: no remote copies, remote signals or barrier semaphores. Data moves between devices by JAX's collectives and lax.ppermute only.
A program may use at most 128 MiB of HBM per device.

```python
import math
import jax
import jax.numpy as jnp
import numpy as np
from jax import lax

HEADS = 24
HEAD_DIM = 128
TILE = 128
DOC_MOST = 4
ROW_TOK = 2048
TILES = 16
DOCS = 5
TOKENS = 65536
N_DP = 32


def draw_query_in(key, part):
    key = jax.random.fold_in(key, 11)
    draw_shape = (TOKENS // TILE, TILE, HEADS * HEAD_DIM)
    drawn = jnp.clip(jax.random.normal(key, draw_shape, jnp.float32), -6.0, 6.0)
    return drawn.reshape(TOKENS, HEADS * HEAD_DIM).astype(jnp.bfloat16)


def draw_key_in(key, part):
    key = jax.random.fold_in(key, 13)
    draw_shape = (TOKENS // TILE, TILE, HEADS * HEAD_DIM)
    drawn = jnp.clip(jax.random.normal(key, draw_shape, jnp.float32), -6.0, 6.0)
    return drawn.reshape(TOKENS, HEADS * HEAD_DIM).astype(jnp.bfloat16)


def draw_packing(key, part):
    key = jax.random.fold_in(key, 23)
    offset_key, rank_key, slot_key = jax.random.split(key, 3)
    offsets = jax.random.permutation(offset_key, N_DP)
    rank_order = jax.random.permutation(rank_key, N_DP)

    def slot_perm(sub_key):
        return jax.random.permutation(sub_key, TILES)
    slot_order = jax.vmap(slot_perm)(jax.random.split(slot_key, N_DP))
    anchor = jnp.arange(N_DP, dtype=jnp.int32)[:, None]
    tile_index = jnp.arange(TILES, dtype=jnp.int32)[None, :]
    target = rank_order[(anchor + offsets[tile_index % N_DP]) % N_DP]
    slot_index = slot_order[target, jnp.broadcast_to(tile_index, target.shape)]
    return (target * TILES + slot_index).reshape(N_DP * TILES).astype(jnp.int32)


def shard_levels(stream_key, extent, cuts, least, largest):
    factor_of, own = 1.0, jax.random.fold_in(stream_key, 6)
    for dim, blocks in cuts:
        heights = jnp.exp(jax.random.uniform(jax.random.fold_in(own, dim), (blocks,), jnp.float32, least / len(cuts), largest / len(cuts)))
        factor_of = factor_of * jnp.repeat(heights, extent[dim] // blocks).reshape([-1 if axis == dim else 1 for axis in range(len(extent))])
    return factor_of


def length_profile(amount, total, bound, lean):
    weights = [(1 << 20) // math.isqrt(grade ** lean) + 1 for grade in range(2, amount + 1)]
    rest, given = total - bound - (amount - 1), [1] * (amount - 1)
    while rest > 0:
        candidates = [i for i in range(amount - 1) if given[i] < bound]
        mass, budget = sum([weights[i] for i in candidates]), rest
        for i in candidates:
            extra = min(bound - given[i], max(1, budget * weights[i] // mass), rest)
            given[i] = given[i] + extra
            rest = rest - extra
    return np.array([bound] + given)


def uneven_parts(rng, count, total, reach, skew):
    if count == 2:
        one = jax.random.randint(rng, (), max(1, total - reach), min(reach, total - 1) + 1)
        return jnp.stack([one, total - one])
    sizes = jnp.asarray(length_profile(count, total, reach, skew), jnp.int32)
    pairs = (count - 1) // 2
    giver, receiver = sizes[1:1 + 2 * pairs:2], sizes[2:2 + 2 * pairs:2]
    slack = jnp.minimum(giver - 1, reach - receiver)
    shifted = jax.random.randint(jax.random.fold_in(rng, 1), (pairs,), 0, 1 << 20) % (slack + 1)
    sizes = sizes.at[1:1 + 2 * pairs:2].set(giver - shifted).at[2:2 + 2 * pairs:2].set(receiver + shifted)
    return sizes[jax.random.permutation(jax.random.fold_in(rng, 2), count)]


def centred(stream_key, dims, spread, limit, pieces=(), held_as=jnp.bfloat16):
    result = jax.random.normal(stream_key, dims, jnp.float32) * spread
    if len(pieces) > 0:
        result = shard_levels(stream_key, dims, pieces, -0.22, 0.18) * result
    return jnp.clip(result, min=-limit, max=limit).astype(held_as)


def setup_inputs(seed: int = 0) -> dict:
    splits = jax.random.split(jax.random.key(seed), 7)
    return {
        "query_in": draw_query_in(jax.random.fold_in(splits[6], 71), 0),
        "key_in": draw_key_in(jax.random.fold_in(splits[6], 71), 0),
        "value_in": centred(splits[2], (TOKENS, HEADS * HEAD_DIM), 1.0, 6.0, ((0, 256),)),
        "grad_out": centred(splits[3], (TOKENS, HEADS * HEAD_DIM), 1.0, 6.0, ((0, 32), (1, 8))),
        "packing": draw_packing(jax.random.fold_in(splits[6], 71), 0),
        "doc_tiles": jax.vmap(lambda own: uneven_parts(own, DOCS, TILES, DOC_MOST, 2))(jax.random.split(splits[5], N_DP)).reshape((N_DP, DOCS)).astype(jnp.int32),
    }


def tile_documents(doc_tiles):
    bounds = jnp.cumsum(doc_tiles, axis=1, dtype=jnp.int32)
    tile_index = jnp.arange(TILES, dtype=jnp.int32)
    per_tile = jnp.sum((bounds[:, None, :] <= tile_index[None, :, None]).astype(jnp.int32), axis=2, dtype=jnp.int32)
    return jnp.repeat(per_tile, TILE, axis=1)


def head_pass(query_rows, key_rows, value_rows, grad_rows, row_docs):
    position = jnp.arange(query_rows.shape[0], dtype=jnp.int32)
    allowed = (row_docs[:, None] == row_docs[None, :]) & (position[:, None] >= position[None, :])
    score_scale = HEAD_DIM ** -0.5
    scores = jnp.dot(query_rows, key_rows.T, preferred_element_type=jnp.float32) * score_scale
    scores = jnp.where(allowed, scores, -jnp.inf)
    row_top = jnp.max(scores, axis=1, keepdims=True)
    weights = jnp.exp(scores - row_top)
    softmax_probs = weights / jnp.sum(weights, axis=1, keepdims=True)
    probs_low = softmax_probs.astype(jnp.bfloat16)
    attended = jnp.dot(probs_low, value_rows, preferred_element_type=jnp.float32).astype(jnp.bfloat16)
    row_delta = jnp.sum(grad_rows.astype(jnp.float32) * attended.astype(jnp.float32), axis=1, keepdims=True)
    grad_value = jnp.dot(probs_low.T, grad_rows, preferred_element_type=jnp.float32).astype(jnp.bfloat16)
    grad_probs = jnp.dot(grad_rows, value_rows.T, preferred_element_type=jnp.float32)
    grad_scores = (softmax_probs * (grad_probs - row_delta) * score_scale).astype(jnp.bfloat16)
    grad_query = jnp.dot(grad_scores, key_rows, preferred_element_type=jnp.float32).astype(jnp.bfloat16)
    grad_key = jnp.dot(grad_scores.T, query_rows, preferred_element_type=jnp.float32).astype(jnp.bfloat16)
    return attended, grad_query, grad_key, grad_value


def heads_first(packed):
    return packed.transpose(1, 0, 2)


def reference(query_in, key_in, value_in, grad_out, packing, doc_tiles):
    row_width = HEADS * HEAD_DIM
    tile_count = N_DP * TILES
    inverse = jnp.zeros((tile_count,), jnp.int32).at[packing].set(jnp.arange(tile_count, dtype=jnp.int32))

    def to_packed(source):
        return source.reshape(tile_count, TILE, row_width)[inverse].reshape(N_DP, ROW_TOK, HEADS, HEAD_DIM)

    def to_anchor(packed):
        return packed.reshape(tile_count, TILE, row_width)[packing].reshape(N_DP * ROW_TOK, row_width)

    doc_of = tile_documents(doc_tiles)
    query_packed = to_packed(query_in)
    key_packed = to_packed(key_in)
    value_packed = to_packed(value_in)
    grad_packed = grad_out.reshape(N_DP, ROW_TOK, HEADS, HEAD_DIM)

    def one_row(row_items):
        query_rows, key_rows, value_rows, grad_rows, row_docs = row_items

        def one_head(head_items):
            return head_pass(head_items[0], head_items[1], head_items[2], head_items[3], row_docs)

        results = lax.map(one_head, (heads_first(query_rows), heads_first(key_rows), heads_first(value_rows), heads_first(grad_rows)))
        return jax.tree.map(heads_first, results)

    attended, grad_query, grad_key, grad_value = lax.map(one_row, (query_packed, key_packed, value_packed, grad_packed, doc_of))
    attended = attended.reshape(N_DP * ROW_TOK, row_width)
    return attended, to_anchor(grad_query), to_anchor(grad_key), to_anchor(grad_value)
```

```python
import functools
import jax
import jax.numpy as jnp
from jax import lax
from jax.experimental import pallas as pl
from jax.experimental.pallas import tpu as pltpu
from jax.sharding import PartitionSpec as P

HEAD_DIM = 128
TILE = 128
DOC_MOST = 4
ROW_TOK = 2048
TILES = 16
DOCS = 5
PARTS = 3
LOG2E = 1.4426950408889634
DEST, SOURCE, ZPOS, DOCLEN = 0, 16, 32, 33

ANY = pl.BlockSpec(memory_space=pl.ANY)
SMEM = pl.BlockSpec(memory_space=pltpu.SMEM)


def run_copies(copies):
    for copy in copies:
        copy.start()
    for copy in copies:
        copy.wait()


def split_kernel(chunk, n_z, heads, n_after, tab, q, k, v, *rest):
    outs, sem = rest[n_after:-1], rest[-1]
    copies = []
    for shift in range(n_z):
        group = lax.rem(tab[ZPOS] + shift, n_z)
        col = pl.multiple_of((group * heads + chunk) * HEAD_DIM, HEAD_DIM)
        for part, src in enumerate((q, k, v)):
            copies.append(
                pltpu.make_async_copy(
                    src.at[:, pl.ds(col, HEAD_DIM)],
                    outs[shift].at[part],
                    sem.at[shift * PARTS + part],
                )
            )
    run_copies(copies)


def split_heads(chunk, n_z, heads, tab, q, k, v, after):
    rows = q.shape[0]
    piece = jax.ShapeDtypeStruct((PARTS, rows, HEAD_DIM), q.dtype)
    return pl.pallas_call(
        functools.partial(split_kernel, chunk, n_z, heads, len(after)),
        out_shape=[piece] * n_z,
        in_specs=[SMEM] + [ANY] * (3 + len(after)),
        out_specs=[ANY] * n_z,
        scratch_shapes=[pltpu.SemaphoreType.DMA((n_z * PARTS,))],
        cost_estimate=pl.CostEstimate(flops=0, bytes_accessed=4 << 20, transcendentals=0),
    )(tab, q, k, v, *after)


def pack_kernel(n_z, per, tab, *rest):
    pieces, send, sem = rest[:n_z], rest[n_z], rest[-1]
    copies = []
    for shift in range(n_z):
        origin = lax.rem(tab[ZPOS] + n_z - shift, n_z)
        for i in range(per):
            dest = tab[DEST + origin * per + i]
            copies.append(
                pltpu.make_async_copy(
                    pieces[shift].at[:, pl.ds(i * TILE, TILE), :],
                    send.at[dest],
                    sem.at[shift * per + i],
                )
            )
    run_copies(copies)


def pack_tiles(n_dp, tab, pieces):
    n_z = len(pieces)
    per = TILES // n_z
    return pl.pallas_call(
        functools.partial(pack_kernel, n_z, per),
        out_shape=jax.ShapeDtypeStruct((n_dp, PARTS, TILE, HEAD_DIM), pieces[0].dtype),
        in_specs=[SMEM] + [ANY] * n_z,
        out_specs=ANY,
        scratch_shapes=[pltpu.SemaphoreType.DMA((TILES,))],
        cost_estimate=pl.CostEstimate(flops=0, bytes_accessed=4 << 20, transcendentals=0),
    )(tab, *pieces)


def unpack_kernel(n_z, per, tab, got, *rest):
    pieces, sem = rest[:n_z], rest[-1]
    copies = []
    for shift in range(n_z):
        target = lax.rem(tab[ZPOS] + shift, n_z)
        for i in range(per):
            dest = tab[DEST + target * per + i]
            copies.append(
                pltpu.make_async_copy(
                    got.at[dest],
                    pieces[shift].at[:, pl.ds(i * TILE, TILE), :],
                    sem.at[shift * per + i],
                )
            )
    run_copies(copies)


def unpack_tiles(n_z, tab, got):
    per = TILES // n_z
    piece = jax.ShapeDtypeStruct((PARTS, per * TILE, HEAD_DIM), got.dtype)
    return pl.pallas_call(
        functools.partial(unpack_kernel, n_z, per),
        out_shape=[piece] * n_z,
        in_specs=[SMEM, ANY],
        out_specs=[ANY] * n_z,
        scratch_shapes=[pltpu.SemaphoreType.DMA((TILES,))],
        cost_estimate=pl.CostEstimate(flops=0, bytes_accessed=4 << 20, transcendentals=0),
    )(tab, got)


def join_kernel(chunk, n_z, heads, n_prev, tab, *rest):
    pieces, outs, sem = rest[:n_z], rest[n_z + n_prev : -1], rest[-1]
    copies = []
    for shift in range(n_z):
        group = lax.rem(tab[ZPOS] + n_z - shift, n_z)
        col = pl.multiple_of((group * heads + chunk) * HEAD_DIM, HEAD_DIM)
        for part in range(PARTS):
            copies.append(
                pltpu.make_async_copy(
                    pieces[shift].at[part],
                    outs[part].at[:, pl.ds(col, HEAD_DIM)],
                    sem.at[shift * PARTS + part],
                )
            )
    run_copies(copies)


def join_heads(chunk, n_z, heads, tab, pieces, prev):
    rows = pieces[0].shape[1]
    out = jax.ShapeDtypeStruct((rows, n_z * heads * HEAD_DIM), pieces[0].dtype)
    return pl.pallas_call(
        functools.partial(join_kernel, chunk, n_z, heads, len(prev)),
        out_shape=[out] * PARTS,
        in_specs=[SMEM] + [ANY] * (n_z + len(prev)),
        out_specs=[ANY] * PARTS,
        scratch_shapes=[pltpu.SemaphoreType.DMA((n_z * PARTS,))],
        input_output_aliases={1 + n_z + i: i for i in range(len(prev))},
        cost_estimate=pl.CostEstimate(flops=0, bytes_accessed=4 << 20, transcendentals=0),
    )(tab, *pieces, *prev)


def attend_kernel(n_prev, tab, grad, got, *rest):
    att, back, tiles, grads, in_sem, out_sem = rest[n_prev:]
    scale = HEAD_DIM ** (-0.5)
    nt = (((1,), (1,)), ((), ()))
    tn = (((0,), (0,)), ((), ()))
    nn = (((1,), (0,)), ((), ()))

    def dot(a, b, dims):
        return lax.dot_general(a, b, dims, preferred_element_type=jnp.float32)

    run_copies(
        [
            pltpu.make_async_copy(
                got.at[tab[SOURCE + t]], tiles.at[:, pl.ds(t * TILE, TILE), :], in_sem.at[t]
            )
            for t in range(TILES)
        ]
    )

    def document(first, count):
        extent = count * TILE
        rows = pl.ds(pl.multiple_of(first * TILE, TILE), extent)
        q, k, v = tiles[0, rows, :], tiles[1, rows, :], tiles[2, rows, :]
        g = grad[rows, :]
        scores = dot(q, k, nt)
        later = lax.broadcasted_iota(jnp.int32, (extent, extent), 0)
        earlier = lax.broadcasted_iota(jnp.int32, (extent, extent), 1)
        scores = jnp.where(later >= earlier, scores, -jnp.inf)
        top = jnp.max(scores, axis=1, keepdims=True)
        weights = jnp.exp2((scores - top) * (scale * LOG2E))
        probs = weights * (1.0 / jnp.sum(weights, axis=1, keepdims=True))
        low = probs.astype(jnp.bfloat16)
        attended = dot(low, v, nn).astype(jnp.bfloat16)
        att[rows, :] = attended
        delta = jnp.sum(
            g.astype(jnp.float32) * attended.astype(jnp.float32), axis=1, keepdims=True
        )
        grads[2, rows, :] = dot(low, g, tn).astype(jnp.bfloat16)
        grad_scores = (probs * (dot(g, v, nt) - delta)).astype(jnp.bfloat16)
        grads[0, rows, :] = (dot(grad_scores, k, nn) * scale).astype(jnp.bfloat16)
        grads[1, rows, :] = (dot(grad_scores, q, tn) * scale).astype(jnp.bfloat16)

    def step(j, first):
        count = tab[DOCLEN + j]
        for size in range(1, DOC_MOST + 1):
            pl.when(count == size)(functools.partial(document, first, size))
        return first + count

    lax.fori_loop(0, DOCS, step, jnp.int32(0))
    run_copies(
        [
            pltpu.make_async_copy(
                grads.at[:, pl.ds(t * TILE, TILE), :], back.at[tab[SOURCE + t]], out_sem.at[t]
            )
            for t in range(TILES)
        ]
    )


def attend(chunk, heads, tab, grad_out, got, prev):
    column = pl.BlockSpec((ROW_TOK, HEAD_DIM), lambda i: (0, chunk))
    return pl.pallas_call(
        functools.partial(attend_kernel, len(prev)),
        grid=(1,),
        out_shape=[
            jax.ShapeDtypeStruct(grad_out.shape, grad_out.dtype),
            jax.ShapeDtypeStruct(got.shape, got.dtype),
        ],
        in_specs=[SMEM, column, ANY] + [ANY] * len(prev),
        out_specs=[column, ANY],
        scratch_shapes=[
            pltpu.VMEM((PARTS, ROW_TOK, HEAD_DIM), jnp.bfloat16),
            pltpu.VMEM((PARTS, ROW_TOK, HEAD_DIM), jnp.bfloat16),
            pltpu.SemaphoreType.DMA((TILES,)),
            pltpu.SemaphoreType.DMA((TILES,)),
        ],
        input_output_aliases={3 + i: i for i in range(len(prev))},
        compiler_params=pltpu.CompilerParams(vmem_limit_bytes=40 << 20),
        cost_estimate=pl.CostEstimate(
            flops=2 << 30, bytes_accessed=8 << 20, transcendentals=1 << 20
        ),
    )(tab, grad_out, got, *prev)


def shift_by(pieces, n_z):
    moved = [pieces[0]]
    for shift in range(1, n_z):
        moved.append(
            lax.ppermute(pieces[shift], "ulysses", [(i, (i + shift) % n_z) for i in range(n_z)])
        )
    return moved


def shards(query_in, key_in, value_in, grad_out, packing, doc_tiles):
    n_dp = lax.axis_size("dp")
    n_z = lax.axis_size("ulysses")
    row_index = lax.axis_index("dp")
    heads = grad_out.shape[1] // HEAD_DIM
    dest = lax.dynamic_slice_in_dim(packing, row_index * TILES, TILES) // TILES
    place = row_index * TILES + jnp.arange(TILES, dtype=jnp.int32)
    source_row = jnp.arange(packing.shape[0], dtype=jnp.int32) // TILES
    source = jnp.sum(
        jnp.where(packing[None, :] == place[:, None], source_row[None, :], 0),
        axis=1,
        dtype=jnp.int32,
    )
    tab = jnp.concatenate(
        [dest, source, lax.axis_index("ulysses")[None].astype(jnp.int32), doc_tiles[0]]
    )

    got, sent = [], ()
    for chunk in range(heads):
        pieces = split_heads(chunk, n_z, heads, tab, query_in, key_in, value_in, sent)
        send = pack_tiles(n_dp, tab, shift_by(pieces, n_z))
        sent = (send,)
        got.append(lax.all_to_all(send, "dp", split_axis=0, concat_axis=0, tiled=True))

    back, prev = [], ()
    for chunk in range(heads):
        attended, home = attend(chunk, heads, tab, grad_out, got[chunk], prev)
        prev = (attended,)
        back.append(lax.all_to_all(home, "dp", split_axis=0, concat_axis=0, tiled=True))

    grads = ()
    for chunk in range(heads):
        pieces = shift_by(unpack_tiles(n_z, tab, back[chunk]), n_z)
        grads = tuple(join_heads(chunk, n_z, heads, tab, pieces, grads))
    return (attended,) + grads


def solution(mesh):
    in_specs = (
        P(("dp", "ulysses"), None),
        P(("dp", "ulysses"), None),
        P(("dp", "ulysses"), None),
        P("dp", "ulysses"),
        P(),
        P("dp", None),
    )
    out_specs = (
        P("dp", "ulysses"),
        P(("dp", "ulysses"), None),
        P(("dp", "ulysses"), None),
        P(("dp", "ulysses"), None),
    )
    return jax.shard_map(shards, mesh=mesh, in_specs=in_specs, out_specs=out_specs, check_vma=False)
```

```python
import functools
import jax
import jax.numpy as jnp
from jax import lax
from jax.experimental import pallas as pl
from jax.experimental.pallas import tpu as pltpu
from jax.sharding import PartitionSpec as P

HEAD_DIM = 128
TILE = 128
DOC_MOST = 4
ROW_TOK = 2048
TILES = 16
DOCS = 5
PARTS = 3
LOG2E = 1.4426950408889634
DEST, SOURCE, ZPOS, DOCLEN = 0, 16, 32, 33

ANY = pl.BlockSpec(memory_space=pl.ANY)
SMEM = pl.BlockSpec(memory_space=pltpu.SMEM)


def run_copies(copies):
    for copy in copies:
        copy.start()
    for copy in copies:
        copy.wait()


def run_moves(moves, held, in_sem, out_sem):
    loads, stores = [], []
    for i, (source, target) in enumerate(moves):
        loads.append(pltpu.make_async_copy(source, held.at[i], in_sem.at[i]))
        stores.append(pltpu.make_async_copy(held.at[i], target, out_sem.at[i]))
    for load in loads:
        load.start()
    for load, store in zip(loads, stores):
        load.wait()
        store.start()
    for store in stores:
        store.wait()


def move_scratch(count, *block):
    return [
        pltpu.VMEM((count,) + block, jnp.bfloat16),
        pltpu.SemaphoreType.DMA((count,)),
        pltpu.SemaphoreType.DMA((count,)),
    ]


def split_kernel(chunk, n_z, heads, n_after, tab, q, k, v, *rest):
    outs, scratch = rest[n_after:-3], rest[-3:]
    moves = []
    for shift in range(n_z):
        group = lax.rem(tab[ZPOS] + shift, n_z)
        col = pl.multiple_of((group * heads + chunk) * HEAD_DIM, HEAD_DIM)
        for part, src in enumerate((q, k, v)):
            moves.append((src.at[:, pl.ds(col, HEAD_DIM)], outs[shift].at[part]))
    run_moves(moves, *scratch)


def split_heads(chunk, n_z, heads, tab, q, k, v, after):
    rows = q.shape[0]
    piece = jax.ShapeDtypeStruct((PARTS, rows, HEAD_DIM), q.dtype)
    return pl.pallas_call(
        functools.partial(split_kernel, chunk, n_z, heads, len(after)),
        out_shape=[piece] * n_z,
        in_specs=[SMEM] + [ANY] * (3 + len(after)),
        out_specs=[ANY] * n_z,
        scratch_shapes=move_scratch(n_z * PARTS, rows, HEAD_DIM),
        compiler_params=pltpu.CompilerParams(vmem_limit_bytes=16 << 20),
        cost_estimate=pl.CostEstimate(flops=0, bytes_accessed=4 << 20, transcendentals=0),
    )(tab, q, k, v, *after)


def pack_kernel(n_z, per, tab, *rest):
    pieces, send, scratch = rest[:n_z], rest[n_z], rest[-3:]
    moves = []
    for shift in range(n_z):
        origin = lax.rem(tab[ZPOS] + n_z - shift, n_z)
        for i in range(per):
            dest = tab[DEST + origin * per + i]
            moves.append((pieces[shift].at[:, pl.ds(i * TILE, TILE), :], send.at[dest]))
    run_moves(moves, *scratch)


def pack_tiles(n_dp, tab, pieces):
    n_z = len(pieces)
    per = TILES // n_z
    return pl.pallas_call(
        functools.partial(pack_kernel, n_z, per),
        out_shape=jax.ShapeDtypeStruct((n_dp, PARTS, TILE, HEAD_DIM), pieces[0].dtype),
        in_specs=[SMEM] + [ANY] * n_z,
        out_specs=ANY,
        scratch_shapes=move_scratch(TILES, PARTS, TILE, HEAD_DIM),
        compiler_params=pltpu.CompilerParams(vmem_limit_bytes=16 << 20),
        cost_estimate=pl.CostEstimate(flops=0, bytes_accessed=4 << 20, transcendentals=0),
    )(tab, *pieces)


def unpack_kernel(n_z, per, tab, got, *rest):
    pieces, scratch = rest[:n_z], rest[-3:]
    moves = []
    for shift in range(n_z):
        target = lax.rem(tab[ZPOS] + shift, n_z)
        for i in range(per):
            dest = tab[DEST + target * per + i]
            moves.append((got.at[dest], pieces[shift].at[:, pl.ds(i * TILE, TILE), :]))
    run_moves(moves, *scratch)


def unpack_tiles(n_z, tab, got):
    per = TILES // n_z
    piece = jax.ShapeDtypeStruct((PARTS, per * TILE, HEAD_DIM), got.dtype)
    return pl.pallas_call(
        functools.partial(unpack_kernel, n_z, per),
        out_shape=[piece] * n_z,
        in_specs=[SMEM, ANY],
        out_specs=[ANY] * n_z,
        scratch_shapes=move_scratch(TILES, PARTS, TILE, HEAD_DIM),
        compiler_params=pltpu.CompilerParams(vmem_limit_bytes=16 << 20),
        cost_estimate=pl.CostEstimate(flops=0, bytes_accessed=4 << 20, transcendentals=0),
    )(tab, got)


def join_kernel(chunk, n_z, heads, n_prev, tab, *rest):
    pieces, outs, scratch = rest[:n_z], rest[n_z + n_prev : -3], rest[-3:]
    moves = []
    for shift in range(n_z):
        group = lax.rem(tab[ZPOS] + n_z - shift, n_z)
        col = pl.multiple_of((group * heads + chunk) * HEAD_DIM, HEAD_DIM)
        for part in range(PARTS):
            moves.append((pieces[shift].at[part], outs[part].at[:, pl.ds(col, HEAD_DIM)]))
    run_moves(moves, *scratch)


def join_heads(chunk, n_z, heads, tab, pieces, prev):
    rows = pieces[0].shape[1]
    out = jax.ShapeDtypeStruct((rows, n_z * heads * HEAD_DIM), pieces[0].dtype)
    return pl.pallas_call(
        functools.partial(join_kernel, chunk, n_z, heads, len(prev)),
        out_shape=[out] * PARTS,
        in_specs=[SMEM] + [ANY] * (n_z + len(prev)),
        out_specs=[ANY] * PARTS,
        scratch_shapes=move_scratch(n_z * PARTS, rows, HEAD_DIM),
        compiler_params=pltpu.CompilerParams(vmem_limit_bytes=16 << 20),
        input_output_aliases={1 + n_z + i: i for i in range(len(prev))},
        cost_estimate=pl.CostEstimate(flops=0, bytes_accessed=4 << 20, transcendentals=0),
    )(tab, *pieces, *prev)


def attend_kernel(n_prev, tab, grad, got, *rest):
    att, back, tiles, grads, in_sem, out_sem = rest[n_prev:]
    scale = HEAD_DIM ** (-0.5)
    nt = (((1,), (1,)), ((), ()))
    tn = (((0,), (0,)), ((), ()))
    nn = (((1,), (0,)), ((), ()))

    def dot(a, b, dims):
        return lax.dot_general(a, b, dims, preferred_element_type=jnp.float32)

    run_copies(
        [
            pltpu.make_async_copy(
                got.at[tab[SOURCE + t]], tiles.at[:, pl.ds(t * TILE, TILE), :], in_sem.at[t]
            )
            for t in range(TILES)
        ]
    )

    def document(first, count):
        extent = count * TILE
        rows = pl.ds(pl.multiple_of(first * TILE, TILE), extent)
        q, k, v = tiles[0, rows, :], tiles[1, rows, :], tiles[2, rows, :]
        g = grad[rows, :]
        scores = dot(q, k, nt)
        later = lax.broadcasted_iota(jnp.int32, (extent, extent), 0)
        earlier = lax.broadcasted_iota(jnp.int32, (extent, extent), 1)
        scores = jnp.where(later >= earlier, scores, -jnp.inf)
        top = jnp.max(scores, axis=1, keepdims=True)
        weights = jnp.exp2((scores - top) * (scale * LOG2E))
        probs = weights * (1.0 / jnp.sum(weights, axis=1, keepdims=True))
        low = probs.astype(jnp.bfloat16)
        attended = dot(low, v, nn).astype(jnp.bfloat16)
        att[rows, :] = attended
        delta = jnp.sum(
            g.astype(jnp.float32) * attended.astype(jnp.float32), axis=1, keepdims=True
        )
        grads[2, rows, :] = dot(low, g, tn).astype(jnp.bfloat16)
        grad_scores = (probs * (dot(g, v, nt) - delta)).astype(jnp.bfloat16)
        grads[0, rows, :] = (dot(grad_scores, k, nn) * scale).astype(jnp.bfloat16)
        grads[1, rows, :] = (dot(grad_scores, q, tn) * scale).astype(jnp.bfloat16)

    def step(j, first):
        count = tab[DOCLEN + j]
        for size in range(1, DOC_MOST + 1):
            pl.when(count == size)(functools.partial(document, first, size))
        return first + count

    lax.fori_loop(0, DOCS, step, jnp.int32(0))
    run_copies(
        [
            pltpu.make_async_copy(
                grads.at[:, pl.ds(t * TILE, TILE), :], back.at[tab[SOURCE + t]], out_sem.at[t]
            )
            for t in range(TILES)
        ]
    )


def attend(chunk, heads, tab, grad_out, got, prev):
    column = pl.BlockSpec((ROW_TOK, HEAD_DIM), lambda i: (0, chunk))
    return pl.pallas_call(
        functools.partial(attend_kernel, len(prev)),
        grid=(1,),
        out_shape=[
            jax.ShapeDtypeStruct(grad_out.shape, grad_out.dtype),
            jax.ShapeDtypeStruct(got.shape, got.dtype),
        ],
        in_specs=[SMEM, column, ANY] + [ANY] * len(prev),
        out_specs=[column, ANY],
        scratch_shapes=[
            pltpu.VMEM((PARTS, ROW_TOK, HEAD_DIM), jnp.bfloat16),
            pltpu.VMEM((PARTS, ROW_TOK, HEAD_DIM), jnp.bfloat16),
            pltpu.SemaphoreType.DMA((TILES,)),
            pltpu.SemaphoreType.DMA((TILES,)),
        ],
        input_output_aliases={3 + i: i for i in range(len(prev))},
        compiler_params=pltpu.CompilerParams(vmem_limit_bytes=40 << 20),
        cost_estimate=pl.CostEstimate(
            flops=2 << 30, bytes_accessed=8 << 20, transcendentals=1 << 20
        ),
    )(tab, grad_out, got, *prev)


def shift_by(pieces, n_z):
    moved = [pieces[0]]
    for shift in range(1, n_z):
        moved.append(
            lax.ppermute(pieces[shift], "ulysses", [(i, (i + shift) % n_z) for i in range(n_z)])
        )
    return moved


def shards(query_in, key_in, value_in, grad_out, packing, doc_tiles):
    n_dp = lax.axis_size("dp")
    n_z = lax.axis_size("ulysses")
    row_index = lax.axis_index("dp")
    heads = grad_out.shape[1] // HEAD_DIM
    dest = lax.dynamic_slice_in_dim(packing, row_index * TILES, TILES) // TILES
    place = row_index * TILES + jnp.arange(TILES, dtype=jnp.int32)
    source_row = jnp.arange(packing.shape[0], dtype=jnp.int32) // TILES
    source = jnp.sum(
        jnp.where(packing[None, :] == place[:, None], source_row[None, :], 0),
        axis=1,
        dtype=jnp.int32,
    )
    tab = jnp.concatenate(
        [dest, source, lax.axis_index("ulysses")[None].astype(jnp.int32), doc_tiles[0]]
    )

    got, sent = [], ()
    for chunk in range(heads):
        pieces = split_heads(chunk, n_z, heads, tab, query_in, key_in, value_in, sent)
        send = pack_tiles(n_dp, tab, shift_by(pieces, n_z))
        sent = (send,)
        got.append(lax.all_to_all(send, "dp", split_axis=0, concat_axis=0, tiled=True))

    back, prev = [], ()
    for chunk in range(heads):
        attended, home = attend(chunk, heads, tab, grad_out, got[chunk], prev)
        prev = (attended,)
        back.append(lax.all_to_all(home, "dp", split_axis=0, concat_axis=0, tiled=True))

    grads = ()
    for chunk in range(heads):
        pieces = shift_by(unpack_tiles(n_z, tab, back[chunk]), n_z)
        grads = tuple(join_heads(chunk, n_z, heads, tab, pieces, grads))
    return (attended,) + grads


def solution(mesh):
    in_specs = (
        P(("dp", "ulysses"), None),
        P(("dp", "ulysses"), None),
        P(("dp", "ulysses"), None),
        P("dp", "ulysses"),
        P(),
        P("dp", None),
    )
    out_specs = (
        P("dp", "ulysses"),
        P(("dp", "ulysses"), None),
        P(("dp", "ulysses"), None),
        P(("dp", "ulysses"), None),
    )
    return jax.shard_map(shards, mesh=mesh, in_specs=in_specs, out_specs=out_specs, check_vma=False)
```

```python
import functools
import jax
import jax.numpy as jnp
from jax import lax
from jax.experimental import pallas as pl
from jax.experimental.pallas import tpu as pltpu
from jax.sharding import PartitionSpec as P

HEAD_DIM = 128
TILE = 128
DOC_MOST = 4
ROW_TOK = 2048
TILES = 16
DOCS = 5
PARTS = 3
LOG2E = 1.4426950408889634
DEST, SOURCE, ZPOS, DOCLEN = 0, 16, 32, 33

HBM = pl.BlockSpec(memory_space=pltpu.HBM)
SMEM = pl.BlockSpec(memory_space=pltpu.SMEM)


def shift_order(n_z):
    order = [0]
    for step in range(n_z // 2 - 1, 0, -1):
        order += [step, n_z - step]
    return order[:3] + [n_z // 2] + order[3:]


def copy_cost(rows):
    return pl.CostEstimate(flops=0, bytes_accessed=4 * rows * HEAD_DIM, transcendentals=0)


def run_copies(copies):
    for copy in copies:
        copy.start()
    for copy in copies:
        copy.wait()


def run_moves(moves, held, in_sem, out_sem):
    loads, stores = [], []
    for i, (source, target) in enumerate(moves):
        loads.append(pltpu.make_async_copy(source, held.at[i], in_sem.at[i]))
        stores.append(pltpu.make_async_copy(held.at[i], target, out_sem.at[i]))
    for load in loads:
        load.start()
    for load, store in zip(loads, stores):
        load.wait()
        store.start()
    for store in stores:
        store.wait()


def move_scratch(count, *block):
    return [
        pltpu.VMEM((count,) + block, jnp.bfloat16),
        pltpu.SemaphoreType.DMA((count,)),
        pltpu.SemaphoreType.DMA((count,)),
    ]


def split_kernel(units, n_z, heads, n_after, tab, q, k, v, *rest):
    outs, scratch = rest[n_after:-3], rest[-3:]
    moves = []
    for u, unit in enumerate(units):
        for place, shift in enumerate(shift_order(n_z)):
            group = lax.rem(tab[ZPOS] + shift, n_z)
            for i, (part, head) in enumerate(unit):
                col = pl.multiple_of((group * heads + head) * HEAD_DIM, HEAD_DIM)
                moves.append(
                    ((q, k, v)[part].at[:, pl.ds(col, HEAD_DIM)], outs[u * n_z + place].at[i])
                )
    run_moves(moves, *scratch)


def split_heads(units, n_z, heads, tab, q, k, v, after):
    rows = q.shape[0]
    count = n_z * sum(len(unit) for unit in units)
    pieces = pl.pallas_call(
        functools.partial(split_kernel, units, n_z, heads, len(after)),
        out_shape=[
            jax.ShapeDtypeStruct((len(unit), rows, HEAD_DIM), q.dtype)
            for unit in units
            for _ in range(n_z)
        ],
        in_specs=[SMEM] + [HBM] * (3 + len(after)),
        out_specs=[HBM] * (n_z * len(units)),
        scratch_shapes=move_scratch(count, rows, HEAD_DIM),
        compiler_params=pltpu.CompilerParams(vmem_limit_bytes=16 << 20),
        cost_estimate=copy_cost(count * rows),
    )(tab, q, k, v, *after)
    return [pieces[u * n_z : (u + 1) * n_z] for u in range(len(units))]


def pack_kernel(n_z, per, n_after, tab, *rest):
    pieces, send, scratch = rest[:n_z], rest[n_z + n_after], rest[-3:]
    moves = []
    for place, shift in enumerate(shift_order(n_z)):
        origin = lax.rem(tab[ZPOS] + n_z - shift, n_z)
        for i in range(per):
            dest = tab[DEST + origin * per + i]
            moves.append((pieces[place].at[:, pl.ds(i * TILE, TILE), :], send.at[dest]))
    run_moves(moves, *scratch)


def pack_tiles(n_dp, tab, pieces, after):
    n_z = len(pieces)
    per = TILES // n_z
    pairs = pieces[0].shape[0]
    return pl.pallas_call(
        functools.partial(pack_kernel, n_z, per, len(after)),
        out_shape=jax.ShapeDtypeStruct((n_dp, pairs, TILE, HEAD_DIM), pieces[0].dtype),
        in_specs=[SMEM] + [HBM] * (n_z + len(after)),
        out_specs=HBM,
        scratch_shapes=move_scratch(TILES, pairs, TILE, HEAD_DIM),
        compiler_params=pltpu.CompilerParams(vmem_limit_bytes=16 << 20),
        cost_estimate=copy_cost(pairs * ROW_TOK),
    )(tab, *pieces, *after)


def unpack_kernel(n_z, per, tab, got, *rest):
    pieces, scratch = rest[:n_z], rest[-3:]
    moves = []
    for place, shift in enumerate(shift_order(n_z)):
        target = lax.rem(tab[ZPOS] + shift, n_z)
        for i in range(per):
            dest = tab[DEST + target * per + i]
            moves.append((got.at[dest], pieces[place].at[:, pl.ds(i * TILE, TILE), :]))
    run_moves(moves, *scratch)


def unpack_tiles(n_z, tab, got):
    per = TILES // n_z
    pairs = got.shape[1]
    piece = jax.ShapeDtypeStruct((pairs, per * TILE, HEAD_DIM), got.dtype)
    return pl.pallas_call(
        functools.partial(unpack_kernel, n_z, per),
        out_shape=[piece] * n_z,
        in_specs=[SMEM, HBM],
        out_specs=[HBM] * n_z,
        scratch_shapes=move_scratch(TILES, pairs, TILE, HEAD_DIM),
        compiler_params=pltpu.CompilerParams(vmem_limit_bytes=16 << 20),
        cost_estimate=copy_cost(pairs * ROW_TOK),
    )(tab, got)


def join_kernel(unit, n_z, heads, n_prev, tab, *rest):
    pieces, outs, scratch = rest[:n_z], rest[n_z + n_prev : -3], rest[-3:]
    moves = []
    for place, shift in enumerate(shift_order(n_z)):
        group = lax.rem(tab[ZPOS] + n_z - shift, n_z)
        for i, (part, head) in enumerate(unit):
            col = pl.multiple_of((group * heads + head) * HEAD_DIM, HEAD_DIM)
            moves.append((pieces[place].at[i], outs[part].at[:, pl.ds(col, HEAD_DIM)]))
    run_moves(moves, *scratch)


def join_heads(unit, n_z, heads, tab, pieces, prev):
    rows = pieces[0].shape[1]
    out = jax.ShapeDtypeStruct((rows, n_z * heads * HEAD_DIM), pieces[0].dtype)
    return pl.pallas_call(
        functools.partial(join_kernel, unit, n_z, heads, len(prev)),
        out_shape=[out] * PARTS,
        in_specs=[SMEM] + [HBM] * (n_z + len(prev)),
        out_specs=[HBM] * PARTS,
        scratch_shapes=move_scratch(n_z * len(unit), rows, HEAD_DIM),
        input_output_aliases={1 + n_z + i: i for i in range(len(prev))},
        compiler_params=pltpu.CompilerParams(vmem_limit_bytes=16 << 20),
        cost_estimate=copy_cost(n_z * len(unit) * rows),
    )(tab, *pieces, *prev)


def gate_kernel(count, *refs):
    pass


def gate(pieces, after):
    count = len(pieces)
    return pl.pallas_call(
        functools.partial(gate_kernel, count),
        out_shape=[jax.ShapeDtypeStruct(piece.shape, piece.dtype) for piece in pieces],
        in_specs=[HBM] * (count + len(after)),
        out_specs=[HBM] * count,
        input_output_aliases={i: i for i in range(count)},
        cost_estimate=pl.CostEstimate(flops=0, bytes_accessed=0, transcendentals=0),
    )(*pieces, *after)


def attend_kernel(got_at, back_at, n_got, n_back, n_after, tab, grad, *rest):
    got, rest = rest[:n_got], rest[n_got + n_after :]
    att, back, rest = rest[0], rest[1 : 1 + n_back], rest[1 + n_back :]
    tiles, grads, in_sem, out_sem = rest
    scale = HEAD_DIM ** (-0.5)
    nt = (((1,), (1,)), ((), ()))
    tn = (((0,), (0,)), ((), ()))
    nn = (((1,), (0,)), ((), ()))

    def dot(a, b, dims):
        return lax.dot_general(a, b, dims, preferred_element_type=jnp.float32)

    run_copies(
        [
            pltpu.make_async_copy(
                got[u].at[tab[SOURCE + t], i],
                tiles.at[part, pl.ds(t * TILE, TILE), :],
                in_sem.at[t * PARTS + part],
            )
            for t in range(TILES)
            for part, (u, i) in enumerate(got_at)
        ]
    )

    def document(first, count):
        extent = count * TILE
        rows = pl.ds(pl.multiple_of(first * TILE, TILE), extent)
        q, k, v = tiles[0, rows, :], tiles[1, rows, :], tiles[2, rows, :]
        g = grad[rows, :]
        scores = dot(q, k, nt)
        later = lax.broadcasted_iota(jnp.int32, (extent, extent), 0)
        earlier = lax.broadcasted_iota(jnp.int32, (extent, extent), 1)
        scores = jnp.where(later >= earlier, scores, -jnp.inf)
        top = jnp.max(scores, axis=1, keepdims=True)
        weights = jnp.exp2((scores - top) * (scale * LOG2E))
        probs = weights * (1.0 / jnp.sum(weights, axis=1, keepdims=True))
        low = probs.astype(jnp.bfloat16)
        attended = dot(low, v, nn).astype(jnp.bfloat16)
        att[rows, :] = attended
        delta = jnp.sum(
            g.astype(jnp.float32) * attended.astype(jnp.float32), axis=1, keepdims=True
        )
        grads[2, rows, :] = dot(low, g, tn).astype(jnp.bfloat16)
        grad_scores = (probs * (dot(g, v, nt) - delta)).astype(jnp.bfloat16)
        grads[0, rows, :] = (dot(grad_scores, k, nn) * scale).astype(jnp.bfloat16)
        grads[1, rows, :] = (dot(grad_scores, q, tn) * scale).astype(jnp.bfloat16)

    def step(j, first):
        count = tab[DOCLEN + j]
        for size in range(1, DOC_MOST + 1):
            pl.when(count == size)(functools.partial(document, first, size))
        return first + count

    lax.fori_loop(0, DOCS, step, jnp.int32(0))
    run_copies(
        [
            pltpu.make_async_copy(
                grads.at[part, pl.ds(t * TILE, TILE), :],
                back[u].at[tab[SOURCE + t], i],
                out_sem.at[t * PARTS + part],
            )
            for t in range(TILES)
            for part, (u, i) in enumerate(back_at)
        ]
    )


def attend(head, tab, grad_out, got, got_at, back_pairs, back_at, prev, after):
    column = pl.BlockSpec((ROW_TOK, HEAD_DIM), lambda i: (0, head))
    slots = got[0].shape[0]
    n_got, n_after = len(got), len(after)
    return pl.pallas_call(
        functools.partial(
            attend_kernel, got_at, back_at, n_got, len(back_pairs), n_after + len(prev)
        ),
        grid=(1,),
        out_shape=[jax.ShapeDtypeStruct(grad_out.shape, grad_out.dtype)]
        + [
            jax.ShapeDtypeStruct((slots, pairs, TILE, HEAD_DIM), grad_out.dtype)
            for pairs in back_pairs
        ],
        in_specs=[SMEM, column] + [HBM] * (n_got + n_after + len(prev)),
        out_specs=[column] + [HBM] * len(back_pairs),
        scratch_shapes=[
            pltpu.VMEM((PARTS, ROW_TOK, HEAD_DIM), jnp.bfloat16),
            pltpu.VMEM((PARTS, ROW_TOK, HEAD_DIM), jnp.bfloat16),
            pltpu.SemaphoreType.DMA((TILES * PARTS,)),
            pltpu.SemaphoreType.DMA((TILES * PARTS,)),
        ],
        input_output_aliases={2 + n_got + n_after + i: i for i in range(len(prev))},
        compiler_params=pltpu.CompilerParams(vmem_limit_bytes=40 << 20),
        cost_estimate=pl.CostEstimate(
            flops=4 << 30, bytes_accessed=8 << 20, transcendentals=4 << 20
        ),
    )(tab, grad_out, *got, *after, *prev)


def shift_by(pieces, n_z):
    moved = []
    for piece, shift in zip(pieces, shift_order(n_z)):
        if shift:
            pairs = [(i, (i + shift) % n_z) for i in range(n_z)]
            piece = lax.ppermute(piece, "ulysses", pairs)
        moved.append(piece)
    return moved


def swap_rows(send):
    return lax.all_to_all(send, "dp", split_axis=0, concat_axis=0, tiled=True)


def shards(query_in, key_in, value_in, grad_out, packing, doc_tiles):
    n_dp = lax.axis_size("dp")
    n_z = lax.axis_size("ulysses")
    row_index = lax.axis_index("dp")
    heads = grad_out.shape[1] // HEAD_DIM
    dest = lax.dynamic_slice_in_dim(packing, row_index * TILES, TILES) // TILES
    place = row_index * TILES + jnp.arange(TILES, dtype=jnp.int32)
    source_row = jnp.arange(packing.shape[0], dtype=jnp.int32) // TILES
    source = jnp.sum(
        jnp.where(packing[None, :] == place[:, None], source_row[None, :], 0),
        axis=1,
        dtype=jnp.int32,
    )
    tab = jnp.concatenate(
        [dest, source, lax.axis_index("ulysses")[None].astype(jnp.int32), doc_tiles[0]]
    )

    whole = [[(part, head) for part in range(PARTS)] for head in range(heads)]
    ins = [whole[0][:1], whole[0][1:]] + whole[1:]
    outs = whole[:-1] + [whole[-1][1:], whole[-1][:1]]

    first = split_heads(ins[:1], n_z, heads, tab, query_in, key_in, value_in, ())
    later = split_heads(ins[1:], n_z, heads, tab, query_in, key_in, value_in, (first[0][0],))
    ready = first + later
    got = []
    pieces = shift_by(ready[0], n_z)
    for u in range(len(ins)):
        here = pieces
        after = ()
        if u + 1 < len(ins):
            gated = gate(ready[u + 1], here)
            after = (gated[0],)
            pieces = shift_by(gated, n_z)
        got.append(swap_rows(pack_tiles(n_dp, tab, here, after)))

    def places(units, head):
        used = [u for u, unit in enumerate(units) if any(h == head for _, h in unit)]
        at = [
            next((i, units[u].index((part, head))) for i, u in enumerate(used) if (part, head) in units[u])
            for part in range(PARTS)
        ]
        return used, at

    back, prev, grads = [], (), ()
    moved = []
    for head in range(heads):
        used, got_at = places(ins, head)
        sends, back_at = places(outs, head)
        attended, *home = attend(
            head,
            tab,
            grad_out,
            [got[u] for u in used],
            got_at,
            [len(outs[u]) for u in sends],
            back_at,
            prev,
            tuple(moved[0][:1]) if head == heads - 1 else (),
        )
        prev = (attended,)
        for send in home:
            back.append(swap_rows(send))
            moved.append(unpack_tiles(n_z, tab, back[-1]))
    for unit, pieces in zip(outs, moved):
        grads = tuple(join_heads(unit, n_z, heads, tab, shift_by(pieces, n_z), grads))
    return (attended,) + grads


def solution(mesh):
    in_specs = (
        P(("dp", "ulysses"), None),
        P(("dp", "ulysses"), None),
        P(("dp", "ulysses"), None),
        P("dp", "ulysses"),
        P(),
        P("dp", None),
    )
    out_specs = (
        P("dp", "ulysses"),
        P(("dp", "ulysses"), None),
        P(("dp", "ulysses"), None),
        P(("dp", "ulysses"), None),
    )
    return jax.shard_map(shards, mesh=mesh, in_specs=in_specs, out_specs=out_specs, check_vma=False)
```

```python
import functools
import jax
import jax.numpy as jnp
from jax import lax
from jax.experimental import pallas as pl
from jax.experimental.pallas import tpu as pltpu
from jax.sharding import PartitionSpec as P

HEAD_DIM = 128
TILE = 128
DOC_MOST = 4
ROW_TOK = 2048
TILES = 16
DOCS = 5
PARTS = 3
LOG2E = 1.4426950408889634
DEST, SOURCE, ZPOS, DOCLEN = 0, 16, 32, 33

ANY = pl.BlockSpec(memory_space=pl.ANY)
SMEM = pl.BlockSpec(memory_space=pltpu.SMEM)


def shift_order(n_z):
    order = [0]
    for step in range(n_z // 2 - 1, 0, -1):
        order += [step, n_z - step]
    return order[:3] + [n_z // 2] + order[3:]


def copy_cost(rows):
    return pl.CostEstimate(flops=0, bytes_accessed=4 * rows * HEAD_DIM, transcendentals=0)


def run_copies(copies):
    for copy in copies:
        copy.start()
    for copy in copies:
        copy.wait()


def run_moves(moves, held, in_sem, out_sem):
    loads, stores = [], []
    for i, (source, target) in enumerate(moves):
        loads.append(pltpu.make_async_copy(source, held.at[i], in_sem.at[i]))
        stores.append(pltpu.make_async_copy(held.at[i], target, out_sem.at[i]))
    for load in loads:
        load.start()
    for load, store in zip(loads, stores):
        load.wait()
        store.start()
    for store in stores:
        store.wait()


def move_scratch(count, *block):
    return [
        pltpu.VMEM((count,) + block, jnp.bfloat16),
        pltpu.SemaphoreType.DMA((count,)),
        pltpu.SemaphoreType.DMA((count,)),
    ]


def split_kernel(units, n_z, heads, n_after, tab, q, k, v, *rest):
    outs, scratch = rest[n_after:-3], rest[-3:]
    moves = []
    for u, unit in enumerate(units):
        for place, shift in enumerate(shift_order(n_z)):
            group = lax.rem(tab[ZPOS] + shift, n_z)
            for i, (part, head) in enumerate(unit):
                col = pl.multiple_of((group * heads + head) * HEAD_DIM, HEAD_DIM)
                moves.append(
                    ((q, k, v)[part].at[:, pl.ds(col, HEAD_DIM)], outs[u * n_z + place].at[i])
                )
    run_moves(moves, *scratch)


def split_heads(units, n_z, heads, tab, q, k, v, after):
    rows = q.shape[0]
    count = n_z * sum(len(unit) for unit in units)
    pieces = pl.pallas_call(
        functools.partial(split_kernel, units, n_z, heads, len(after)),
        out_shape=[
            jax.ShapeDtypeStruct((len(unit), rows, HEAD_DIM), q.dtype)
            for unit in units
            for _ in range(n_z)
        ],
        in_specs=[SMEM] + [ANY] * (3 + len(after)),
        out_specs=[ANY] * (n_z * len(units)),
        scratch_shapes=move_scratch(count, rows, HEAD_DIM),
        compiler_params=pltpu.CompilerParams(vmem_limit_bytes=16 << 20),
        cost_estimate=copy_cost(count * rows),
    )(tab, q, k, v, *after)
    return [pieces[u * n_z : (u + 1) * n_z] for u in range(len(units))]


def pack_kernel(n_z, per, n_after, tab, *rest):
    pieces, send, scratch = rest[:n_z], rest[n_z + n_after], rest[-3:]
    moves = []
    for place, shift in enumerate(shift_order(n_z)):
        origin = lax.rem(tab[ZPOS] + n_z - shift, n_z)
        for i in range(per):
            dest = tab[DEST + origin * per + i]
            moves.append((pieces[place].at[:, pl.ds(i * TILE, TILE), :], send.at[dest]))
    run_moves(moves, *scratch)


def pack_tiles(n_dp, tab, pieces, after):
    n_z = len(pieces)
    per = TILES // n_z
    pairs = pieces[0].shape[0]
    return pl.pallas_call(
        functools.partial(pack_kernel, n_z, per, len(after)),
        out_shape=jax.ShapeDtypeStruct((n_dp, pairs, TILE, HEAD_DIM), pieces[0].dtype),
        in_specs=[SMEM] + [ANY] * (n_z + len(after)),
        out_specs=ANY,
        scratch_shapes=move_scratch(TILES, pairs, TILE, HEAD_DIM),
        compiler_params=pltpu.CompilerParams(vmem_limit_bytes=16 << 20),
        cost_estimate=copy_cost(pairs * ROW_TOK),
    )(tab, *pieces, *after)


def unpack_kernel(n_z, per, tab, got, *rest):
    pieces, scratch = rest[:n_z], rest[-3:]
    moves = []
    for place, shift in enumerate(shift_order(n_z)):
        target = lax.rem(tab[ZPOS] + shift, n_z)
        for i in range(per):
            dest = tab[DEST + target * per + i]
            moves.append((got.at[dest], pieces[place].at[:, pl.ds(i * TILE, TILE), :]))
    run_moves(moves, *scratch)


def unpack_tiles(n_z, tab, got):
    per = TILES // n_z
    pairs = got.shape[1]
    piece = jax.ShapeDtypeStruct((pairs, per * TILE, HEAD_DIM), got.dtype)
    return pl.pallas_call(
        functools.partial(unpack_kernel, n_z, per),
        out_shape=[piece] * n_z,
        in_specs=[SMEM, ANY],
        out_specs=[ANY] * n_z,
        scratch_shapes=move_scratch(TILES, pairs, TILE, HEAD_DIM),
        compiler_params=pltpu.CompilerParams(vmem_limit_bytes=16 << 20),
        cost_estimate=copy_cost(pairs * ROW_TOK),
    )(tab, got)


def join_kernel(unit, n_z, heads, n_prev, tab, *rest):
    pieces, outs, scratch = rest[:n_z], rest[n_z + n_prev : -3], rest[-3:]
    moves = []
    for place, shift in enumerate(shift_order(n_z)):
        group = lax.rem(tab[ZPOS] + n_z - shift, n_z)
        for i, (part, head) in enumerate(unit):
            col = pl.multiple_of((group * heads + head) * HEAD_DIM, HEAD_DIM)
            moves.append((pieces[place].at[i], outs[part].at[:, pl.ds(col, HEAD_DIM)]))
    run_moves(moves, *scratch)


def join_heads(unit, n_z, heads, tab, pieces, prev):
    rows = pieces[0].shape[1]
    out = jax.ShapeDtypeStruct((rows, n_z * heads * HEAD_DIM), pieces[0].dtype)
    return pl.pallas_call(
        functools.partial(join_kernel, unit, n_z, heads, len(prev)),
        out_shape=[out] * PARTS,
        in_specs=[SMEM] + [ANY] * (n_z + len(prev)),
        out_specs=[ANY] * PARTS,
        scratch_shapes=move_scratch(n_z * len(unit), rows, HEAD_DIM),
        input_output_aliases={1 + n_z + i: i for i in range(len(prev))},
        compiler_params=pltpu.CompilerParams(vmem_limit_bytes=16 << 20),
        cost_estimate=copy_cost(n_z * len(unit) * rows),
    )(tab, *pieces, *prev)


def attend_kernel(got_at, back_at, n_got, n_back, n_after, tab, grad, *rest):
    got, rest = rest[:n_got], rest[n_got + n_after :]
    att, back, rest = rest[0], rest[1 : 1 + n_back], rest[1 + n_back :]
    tiles, grads, in_sem, out_sem = rest
    scale = HEAD_DIM ** (-0.5)
    nt = (((1,), (1,)), ((), ()))
    tn = (((0,), (0,)), ((), ()))
    nn = (((1,), (0,)), ((), ()))

    def dot(a, b, dims):
        return lax.dot_general(a, b, dims, preferred_element_type=jnp.float32)

    run_copies(
        [
            pltpu.make_async_copy(
                got[u].at[tab[SOURCE + t], i],
                tiles.at[part, pl.ds(t * TILE, TILE), :],
                in_sem.at[t * PARTS + part],
            )
            for t in range(TILES)
            for part, (u, i) in enumerate(got_at)
        ]
    )

    def document(first, count):
        extent = count * TILE
        rows = pl.ds(pl.multiple_of(first * TILE, TILE), extent)
        q, k, v = tiles[0, rows, :], tiles[1, rows, :], tiles[2, rows, :]
        g = grad[rows, :]
        scores = dot(q, k, nt)
        later = lax.broadcasted_iota(jnp.int32, (extent, extent), 0)
        earlier = lax.broadcasted_iota(jnp.int32, (extent, extent), 1)
        scores = jnp.where(later >= earlier, scores, -jnp.inf)
        top = jnp.max(scores, axis=1, keepdims=True)
        weights = jnp.exp2((scores - top) * (scale * LOG2E))
        probs = weights * (1.0 / jnp.sum(weights, axis=1, keepdims=True))
        low = probs.astype(jnp.bfloat16)
        attended = dot(low, v, nn).astype(jnp.bfloat16)
        att[rows, :] = attended
        delta = jnp.sum(
            g.astype(jnp.float32) * attended.astype(jnp.float32), axis=1, keepdims=True
        )
        grads[2, rows, :] = dot(low, g, tn).astype(jnp.bfloat16)
        grad_scores = (probs * (dot(g, v, nt) - delta)).astype(jnp.bfloat16)
        grads[0, rows, :] = (dot(grad_scores, k, nn) * scale).astype(jnp.bfloat16)
        grads[1, rows, :] = (dot(grad_scores, q, tn) * scale).astype(jnp.bfloat16)

    def step(j, first):
        count = tab[DOCLEN + j]
        for size in range(1, DOC_MOST + 1):
            pl.when(count == size)(functools.partial(document, first, size))
        return first + count

    lax.fori_loop(0, DOCS, step, jnp.int32(0))
    run_copies(
        [
            pltpu.make_async_copy(
                grads.at[part, pl.ds(t * TILE, TILE), :],
                back[u].at[tab[SOURCE + t], i],
                out_sem.at[t * PARTS + part],
            )
            for t in range(TILES)
            for part, (u, i) in enumerate(back_at)
        ]
    )


def attend(head, tab, grad_out, got, got_at, back_pairs, back_at, prev, after):
    column = pl.BlockSpec((ROW_TOK, HEAD_DIM), lambda i: (0, head))
    slots = got[0].shape[0]
    n_got, n_after = len(got), len(after)
    return pl.pallas_call(
        functools.partial(
            attend_kernel, got_at, back_at, n_got, len(back_pairs), n_after + len(prev)
        ),
        grid=(1,),
        out_shape=[jax.ShapeDtypeStruct(grad_out.shape, grad_out.dtype)]
        + [
            jax.ShapeDtypeStruct((slots, pairs, TILE, HEAD_DIM), grad_out.dtype)
            for pairs in back_pairs
        ],
        in_specs=[SMEM, column] + [ANY] * (n_got + n_after + len(prev)),
        out_specs=[column] + [ANY] * len(back_pairs),
        scratch_shapes=[
            pltpu.VMEM((PARTS, ROW_TOK, HEAD_DIM), jnp.bfloat16),
            pltpu.VMEM((PARTS, ROW_TOK, HEAD_DIM), jnp.bfloat16),
            pltpu.SemaphoreType.DMA((TILES * PARTS,)),
            pltpu.SemaphoreType.DMA((TILES * PARTS,)),
        ],
        input_output_aliases={2 + n_got + n_after + i: i for i in range(len(prev))},
        compiler_params=pltpu.CompilerParams(vmem_limit_bytes=40 << 20),
        cost_estimate=pl.CostEstimate(
            flops=4 << 30, bytes_accessed=8 << 20, transcendentals=4 << 20
        ),
    )(tab, grad_out, *got, *after, *prev)


def shift_by(pieces, n_z):
    moved = []
    for piece, shift in zip(pieces, shift_order(n_z)):
        if shift:
            pairs = [(i, (i + shift) % n_z) for i in range(n_z)]
            piece = lax.ppermute(piece, "ulysses", pairs)
        moved.append(piece)
    return moved


def swap_rows(send):
    return lax.all_to_all(send, "dp", split_axis=0, concat_axis=0, tiled=True)


def shards(query_in, key_in, value_in, grad_out, packing, doc_tiles):
    n_dp = lax.axis_size("dp")
    n_z = lax.axis_size("ulysses")
    row_index = lax.axis_index("dp")
    heads = grad_out.shape[1] // HEAD_DIM
    dest = lax.dynamic_slice_in_dim(packing, row_index * TILES, TILES) // TILES
    place = row_index * TILES + jnp.arange(TILES, dtype=jnp.int32)
    source_row = jnp.arange(packing.shape[0], dtype=jnp.int32) // TILES
    source = jnp.sum(
        jnp.where(packing[None, :] == place[:, None], source_row[None, :], 0),
        axis=1,
        dtype=jnp.int32,
    )
    tab = jnp.concatenate(
        [dest, source, lax.axis_index("ulysses")[None].astype(jnp.int32), doc_tiles[0]]
    )

    whole = [[(part, head) for part in range(PARTS)] for head in range(heads)]
    ins = outs = whole

    first = split_heads(ins[:1], n_z, heads, tab, query_in, key_in, value_in, ())
    later = split_heads(ins[1:], n_z, heads, tab, query_in, key_in, value_in, (first[0][0],))
    ready = first + later
    sends = [pack_tiles(n_dp, tab, shift_by(pieces, n_z), ()) for pieces in ready]
    got = [swap_rows(send) for send in sends]

    def places(units, head):
        used = [u for u, unit in enumerate(units) if any(h == head for _, h in unit)]
        at = [
            next((i, units[u].index((part, head))) for i, u in enumerate(used) if (part, head) in units[u])
            for part in range(PARTS)
        ]
        return used, at

    back, prev, grads = [], (), ()
    moved = []
    for head in range(heads):
        used, got_at = places(ins, head)
        targets, back_at = places(outs, head)
        attended, *home = attend(
            head,
            tab,
            grad_out,
            [got[u] for u in used],
            got_at,
            [len(outs[u]) for u in targets],
            back_at,
            prev,
            (sends[-1],) if head == 0 else tuple(moved[0][:1]) if head == heads - 1 else (),
        )
        prev = (attended,)
        for send in home:
            back.append(swap_rows(send))
            moved.append(unpack_tiles(n_z, tab, back[-1]))
    for unit, pieces in zip(outs, moved):
        grads = tuple(join_heads(unit, n_z, heads, tab, shift_by(pieces, n_z), grads))
    return (attended,) + grads


def solution(mesh):
    in_specs = (
        P(("dp", "ulysses"), None),
        P(("dp", "ulysses"), None),
        P(("dp", "ulysses"), None),
        P("dp", "ulysses"),
        P(),
        P("dp", None),
    )
    out_specs = (
        P("dp", "ulysses"),
        P(("dp", "ulysses"), None),
        P(("dp", "ulysses"), None),
        P(("dp", "ulysses"), None),
    )
    return jax.shard_map(shards, mesh=mesh, in_specs=in_specs, out_specs=out_specs, check_vma=False)
```

```python
import functools
import jax
import jax.numpy as jnp
from jax import lax
from jax.experimental import pallas as pl
from jax.experimental.pallas import tpu as pltpu
from jax.sharding import PartitionSpec as P

HEAD_DIM = 128
TILE = 128
DOC_MOST = 4
ROW_TOK = 2048
TILES = 16
DOCS = 5
PARTS = 3
LOG2E = 1.4426950408889634
DEST, SOURCE, ZPOS, DOCLEN = 0, 16, 32, 33

ANY = pl.BlockSpec(memory_space=pl.ANY)
SMEM = pl.BlockSpec(memory_space=pltpu.SMEM)


def shift_order(n_z):
    order = [0]
    for step in range(n_z // 2 - 1, 0, -1):
        order += [step, n_z - step]
    return order[:3] + [n_z // 2] + order[3:]


def copy_cost(rows):
    return pl.CostEstimate(flops=0, bytes_accessed=4 * rows * HEAD_DIM, transcendentals=0)


def run_copies(copies):
    for copy in copies:
        copy.start()
    for copy in copies:
        copy.wait()


def run_moves(moves, held, in_sem, out_sem):
    loads, stores = [], []
    for i, (source, target) in enumerate(moves):
        loads.append(pltpu.make_async_copy(source, held.at[i], in_sem.at[i]))
        stores.append(pltpu.make_async_copy(held.at[i], target, out_sem.at[i]))
    for load in loads:
        load.start()
    for load, store in zip(loads, stores):
        load.wait()
        store.start()
    for store in stores:
        store.wait()


def move_scratch(count, *block):
    return [
        pltpu.VMEM((count,) + block, jnp.bfloat16),
        pltpu.SemaphoreType.DMA((count,)),
        pltpu.SemaphoreType.DMA((count,)),
    ]


def split_kernel(unit, n_z, heads, n_after, tab, q, k, v, *rest):
    outs, scratch = rest[n_after:-3], rest[-3:]
    moves = []
    for place, shift in enumerate(shift_order(n_z)):
        group = lax.rem(tab[ZPOS] + shift, n_z)
        for i, (part, head) in enumerate(unit):
            col = pl.multiple_of((group * heads + head) * HEAD_DIM, HEAD_DIM)
            moves.append(((q, k, v)[part].at[:, pl.ds(col, HEAD_DIM)], outs[place].at[i]))
    run_moves(moves, *scratch)


def split_heads(unit, n_z, heads, tab, q, k, v, after):
    rows = q.shape[0]
    return pl.pallas_call(
        functools.partial(split_kernel, unit, n_z, heads, len(after)),
        out_shape=[jax.ShapeDtypeStruct((len(unit), rows, HEAD_DIM), q.dtype)] * n_z,
        in_specs=[SMEM] + [ANY] * (3 + len(after)),
        out_specs=[ANY] * n_z,
        scratch_shapes=move_scratch(n_z * len(unit), rows, HEAD_DIM),
        compiler_params=pltpu.CompilerParams(vmem_limit_bytes=(6 if after else 60) << 20),
        cost_estimate=copy_cost(n_z * len(unit) * rows),
    )(tab, q, k, v, *after)


def pack_kernel(n_z, per, n_after, tab, *rest):
    pieces, send, scratch = rest[:n_z], rest[n_z + n_after], rest[-3:]
    moves = []
    for place, shift in enumerate(shift_order(n_z)):
        origin = lax.rem(tab[ZPOS] + n_z - shift, n_z)
        for i in range(per):
            dest = tab[DEST + origin * per + i]
            moves.append((pieces[place].at[:, pl.ds(i * TILE, TILE), :], send.at[dest]))
    run_moves(moves, *scratch)


def pack_tiles(n_dp, tab, pieces, after):
    n_z = len(pieces)
    per = TILES // n_z
    pairs = pieces[0].shape[0]
    return pl.pallas_call(
        functools.partial(pack_kernel, n_z, per, len(after)),
        out_shape=jax.ShapeDtypeStruct((n_dp, pairs, TILE, HEAD_DIM), pieces[0].dtype),
        in_specs=[SMEM] + [ANY] * (n_z + len(after)),
        out_specs=ANY,
        scratch_shapes=move_scratch(TILES, pairs, TILE, HEAD_DIM),
        compiler_params=pltpu.CompilerParams(vmem_limit_bytes=6 << 20),
        cost_estimate=copy_cost(pairs * ROW_TOK),
    )(tab, *pieces, *after)


def unpack_kernel(n_z, per, n_after, tab, got, *rest):
    pieces, scratch = rest[n_after : n_after + n_z], rest[-3:]
    moves = []
    for place, shift in enumerate(shift_order(n_z)):
        target = lax.rem(tab[ZPOS] + shift, n_z)
        for i in range(per):
            dest = tab[DEST + target * per + i]
            moves.append((got.at[dest], pieces[place].at[:, pl.ds(i * TILE, TILE), :]))
    run_moves(moves, *scratch)


def unpack_tiles(n_z, tab, got, after):
    per = TILES // n_z
    pairs = got.shape[1]
    piece = jax.ShapeDtypeStruct((pairs, per * TILE, HEAD_DIM), got.dtype)
    return pl.pallas_call(
        functools.partial(unpack_kernel, n_z, per, len(after)),
        out_shape=[piece] * n_z,
        in_specs=[SMEM, ANY] + [ANY] * len(after),
        out_specs=[ANY] * n_z,
        scratch_shapes=move_scratch(TILES, pairs, TILE, HEAD_DIM),
        compiler_params=pltpu.CompilerParams(vmem_limit_bytes=6 << 20),
        cost_estimate=copy_cost(pairs * ROW_TOK),
    )(tab, got, *after)


def join_kernel(unit, n_z, heads, n_prev, tab, *rest):
    pieces, outs, scratch = rest[:n_z], rest[n_z + n_prev : -3], rest[-3:]
    moves = []
    for place, shift in enumerate(shift_order(n_z)):
        group = lax.rem(tab[ZPOS] + n_z - shift, n_z)
        for i, (part, head) in enumerate(unit):
            col = pl.multiple_of((group * heads + head) * HEAD_DIM, HEAD_DIM)
            moves.append((pieces[place].at[i], outs[part].at[:, pl.ds(col, HEAD_DIM)]))
    run_moves(moves, *scratch)


def join_heads(unit, n_z, heads, tab, pieces, prev):
    rows = pieces[0].shape[1]
    out = jax.ShapeDtypeStruct((rows, n_z * heads * HEAD_DIM), pieces[0].dtype)
    return pl.pallas_call(
        functools.partial(join_kernel, unit, n_z, heads, len(prev)),
        out_shape=[out] * PARTS,
        in_specs=[SMEM] + [ANY] * (n_z + len(prev)),
        out_specs=[ANY] * PARTS,
        scratch_shapes=move_scratch(n_z * len(unit), rows, HEAD_DIM),
        input_output_aliases={1 + n_z + i: i for i in range(len(prev))},
        compiler_params=pltpu.CompilerParams(vmem_limit_bytes=6 << 20),
        cost_estimate=copy_cost(n_z * len(unit) * rows),
    )(tab, *pieces, *prev)


def attend_kernel(got_at, back_at, n_got, n_back, n_after, tab, grad, *rest):
    got, rest = rest[:n_got], rest[n_got + n_after :]
    att, back, rest = rest[0], rest[1 : 1 + n_back], rest[1 + n_back :]
    tiles, grads, in_sem, out_sem = rest
    scale = HEAD_DIM ** (-0.5)
    nt = (((1,), (1,)), ((), ()))
    tn = (((0,), (0,)), ((), ()))
    nn = (((1,), (0,)), ((), ()))

    def dot(a, b, dims):
        return lax.dot_general(a, b, dims, preferred_element_type=jnp.float32)

    run_copies(
        [
            pltpu.make_async_copy(
                got[u].at[tab[SOURCE + t], i],
                tiles.at[part, pl.ds(t * TILE, TILE), :],
                in_sem.at[t * PARTS + part],
            )
            for t in range(TILES)
            for part, (u, i) in enumerate(got_at)
        ]
    )

    def document(first, count):
        extent = count * TILE
        rows = pl.ds(pl.multiple_of(first * TILE, TILE), extent)
        q, k, v = tiles[0, rows, :], tiles[1, rows, :], tiles[2, rows, :]
        g = grad[rows, :]
        scores = dot(q, k, nt)
        later = lax.broadcasted_iota(jnp.int32, (extent, extent), 0)
        earlier = lax.broadcasted_iota(jnp.int32, (extent, extent), 1)
        scores = jnp.where(later >= earlier, scores, -jnp.inf)
        top = jnp.max(scores, axis=1, keepdims=True)
        weights = jnp.exp2((scores - top) * (scale * LOG2E))
        probs = weights * (1.0 / jnp.sum(weights, axis=1, keepdims=True))
        low = probs.astype(jnp.bfloat16)
        attended = dot(low, v, nn).astype(jnp.bfloat16)
        att[rows, :] = attended
        delta = jnp.sum(
            g.astype(jnp.float32) * attended.astype(jnp.float32), axis=1, keepdims=True
        )
        grads[2, rows, :] = dot(low, g, tn).astype(jnp.bfloat16)
        grad_scores = (probs * (dot(g, v, nt) - delta)).astype(jnp.bfloat16)
        grads[0, rows, :] = (dot(grad_scores, k, nn) * scale).astype(jnp.bfloat16)
        grads[1, rows, :] = (dot(grad_scores, q, tn) * scale).astype(jnp.bfloat16)

    def step(j, first):
        count = tab[DOCLEN + j]
        for size in range(1, DOC_MOST + 1):
            pl.when(count == size)(functools.partial(document, first, size))
        return first + count

    lax.fori_loop(0, DOCS, step, jnp.int32(0))
    run_copies(
        [
            pltpu.make_async_copy(
                grads.at[part, pl.ds(t * TILE, TILE), :],
                back[u].at[tab[SOURCE + t], i],
                out_sem.at[t * PARTS + part],
            )
            for t in range(TILES)
            for part, (u, i) in enumerate(back_at)
        ]
    )


def attend(head, tab, grad_out, got, got_at, back_pairs, back_at, prev, after):
    column = pl.BlockSpec((ROW_TOK, HEAD_DIM), lambda i: (0, head))
    slots = got[0].shape[0]
    n_got, n_after = len(got), len(after)
    return pl.pallas_call(
        functools.partial(
            attend_kernel, got_at, back_at, n_got, len(back_pairs), n_after + len(prev)
        ),
        grid=(1,),
        out_shape=[jax.ShapeDtypeStruct(grad_out.shape, grad_out.dtype)]
        + [
            jax.ShapeDtypeStruct((slots, pairs, TILE, HEAD_DIM), grad_out.dtype)
            for pairs in back_pairs
        ],
        in_specs=[SMEM, column] + [ANY] * (n_got + n_after + len(prev)),
        out_specs=[column] + [ANY] * len(back_pairs),
        scratch_shapes=[
            pltpu.VMEM((PARTS, ROW_TOK, HEAD_DIM), jnp.bfloat16),
            pltpu.VMEM((PARTS, ROW_TOK, HEAD_DIM), jnp.bfloat16),
            pltpu.SemaphoreType.DMA((TILES * PARTS,)),
            pltpu.SemaphoreType.DMA((TILES * PARTS,)),
        ],
        input_output_aliases={2 + n_got + n_after + i: i for i in range(len(prev))},
        compiler_params=pltpu.CompilerParams(vmem_limit_bytes=24 << 20),
        cost_estimate=pl.CostEstimate(
            flops=4 << 30, bytes_accessed=8 << 20, transcendentals=4 << 20
        ),
    )(tab, grad_out, *got, *after, *prev)


def shift_by(pieces, n_z):
    moved = []
    for piece, shift in zip(pieces, shift_order(n_z)):
        if shift:
            pairs = [(i, (i + shift) % n_z) for i in range(n_z)]
            piece = lax.ppermute(piece, "ulysses", pairs)
        moved.append(piece)
    return moved


def swap_rows(send):
    return lax.all_to_all(send, "dp", split_axis=0, concat_axis=0, tiled=True)


def shards(query_in, key_in, value_in, grad_out, packing, doc_tiles):
    n_dp = lax.axis_size("dp")
    n_z = lax.axis_size("ulysses")
    row_index = lax.axis_index("dp")
    heads = grad_out.shape[1] // HEAD_DIM
    dest = lax.dynamic_slice_in_dim(packing, row_index * TILES, TILES) // TILES
    place = row_index * TILES + jnp.arange(TILES, dtype=jnp.int32)
    source_row = jnp.arange(packing.shape[0], dtype=jnp.int32) // TILES
    source = jnp.sum(
        jnp.where(packing[None, :] == place[:, None], source_row[None, :], 0),
        axis=1,
        dtype=jnp.int32,
    )
    tab = jnp.concatenate(
        [dest, source, lax.axis_index("ulysses")[None].astype(jnp.int32), doc_tiles[0]]
    )

    whole = [[(part, head) for part in range(PARTS)] for head in range(heads)]
    ins = outs = whole

    sends, after = [], ()
    for unit in ins:
        pieces = split_heads(unit, n_z, heads, tab, query_in, key_in, value_in, after)
        pieces = shift_by(pieces, n_z)
        after = (pieces[1],)
        sends.append(pack_tiles(n_dp, tab, pieces, ()))
    got = [swap_rows(send) for send in sends]

    def places(units, head):
        used = [u for u, unit in enumerate(units) if any(h == head for _, h in unit)]
        at = [
            next((i, units[u].index((part, head))) for i, u in enumerate(used) if (part, head) in units[u])
            for part in range(PARTS)
        ]
        return used, at

    prev, back, after = (), [], (sends[-1],)
    for head in range(heads):
        used, got_at = places(ins, head)
        targets, back_at = places(outs, head)
        attended, *home = attend(
            head,
            tab,
            grad_out,
            [got[u] for u in used],
            got_at,
            [len(outs[u]) for u in targets],
            back_at,
            prev,
            after if head == 0 else (),
        )
        prev = (attended,)
        back += [swap_rows(send) for send in home]

    moved, after = [], ()
    for arrived in back:
        pieces = shift_by(unpack_tiles(n_z, tab, arrived, after), n_z)
        after = tuple(pieces[1:])
        moved.append(pieces)

    grads = ()
    for unit, pieces in zip(outs, moved):
        grads = tuple(join_heads(unit, n_z, heads, tab, pieces, grads))
    return (attended,) + grads


def solution(mesh):
    in_specs = (
        P(("dp", "ulysses"), None),
        P(("dp", "ulysses"), None),
        P(("dp", "ulysses"), None),
        P("dp", "ulysses"),
        P(),
        P("dp", None),
    )
    out_specs = (
        P("dp", "ulysses"),
        P(("dp", "ulysses"), None),
        P(("dp", "ulysses"), None),
        P(("dp", "ulysses"), None),
    )
    return jax.shard_map(shards, mesh=mesh, in_specs=in_specs, out_specs=out_specs, check_vma=False)
```

```python
import functools
import jax
import jax.numpy as jnp
from jax import lax
from jax.experimental import pallas as pl
from jax.experimental.pallas import tpu as pltpu
from jax.sharding import PartitionSpec as P

HEAD_DIM = 128
TILE = 128
DOC_MOST = 4
ROW_TOK = 2048
TILES = 16
DOCS = 5
PARTS = 3
LOG2E = 1.4426950408889634
DEST, SOURCE, ZPOS, DOCLEN = 0, 16, 32, 33

ANY = pl.BlockSpec(memory_space=pl.ANY)
SMEM = pl.BlockSpec(memory_space=pltpu.SMEM)


def shift_order(n_z):
    order = [0]
    for step in range(n_z // 2 - 1, 0, -1):
        order += [step, n_z - step]
    return order[:3] + [n_z // 2] + order[3:]


def copy_cost(rows):
    return pl.CostEstimate(flops=0, bytes_accessed=4 * rows * HEAD_DIM, transcendentals=0)


def run_copies(copies):
    for copy in copies:
        copy.start()
    for copy in copies:
        copy.wait()


def run_moves(moves, held, in_sem, out_sem):
    loads, stores = [], []
    for i, (source, target) in enumerate(moves):
        loads.append(pltpu.make_async_copy(source, held.at[i], in_sem.at[i]))
        stores.append(pltpu.make_async_copy(held.at[i], target, out_sem.at[i]))
    for load in loads:
        load.start()
    for load, store in zip(loads, stores):
        load.wait()
        store.start()
    for store in stores:
        store.wait()


def move_scratch(count, *block):
    return [
        pltpu.VMEM((count,) + block, jnp.bfloat16),
        pltpu.SemaphoreType.DMA((count,)),
        pltpu.SemaphoreType.DMA((count,)),
    ]


def split_kernel(unit, n_z, heads, n_after, tab, q, k, v, *rest):
    outs, scratch = rest[n_after:-3], rest[-3:]
    moves = []
    for place, shift in enumerate(shift_order(n_z)):
        group = lax.rem(tab[ZPOS] + shift, n_z)
        for i, (part, head) in enumerate(unit):
            col = pl.multiple_of((group * heads + head) * HEAD_DIM, HEAD_DIM)
            moves.append(((q, k, v)[part].at[:, pl.ds(col, HEAD_DIM)], outs[place].at[i]))
    run_moves(moves, *scratch)


def split_heads(unit, n_z, heads, tab, q, k, v, after):
    rows = q.shape[0]
    return pl.pallas_call(
        functools.partial(split_kernel, unit, n_z, heads, len(after)),
        out_shape=[jax.ShapeDtypeStruct((len(unit), rows, HEAD_DIM), q.dtype)] * n_z,
        in_specs=[SMEM] + [ANY] * (3 + len(after)),
        out_specs=[ANY] * n_z,
        scratch_shapes=move_scratch(n_z * len(unit), rows, HEAD_DIM),
        compiler_params=pltpu.CompilerParams(vmem_limit_bytes=(6 if after else 60) << 20),
        cost_estimate=copy_cost(n_z * len(unit) * rows),
    )(tab, q, k, v, *after)


def pack_kernel(n_z, per, n_after, tab, *rest):
    pieces, send, scratch = rest[:n_z], rest[n_z + n_after], rest[-3:]
    moves = []
    for place, shift in enumerate(shift_order(n_z)):
        origin = lax.rem(tab[ZPOS] + n_z - shift, n_z)
        for i in range(per):
            dest = tab[DEST + origin * per + i]
            moves.append((pieces[place].at[:, pl.ds(i * TILE, TILE), :], send.at[dest]))
    run_moves(moves, *scratch)


def pack_tiles(n_dp, tab, pieces, after):
    n_z = len(pieces)
    per = TILES // n_z
    pairs = pieces[0].shape[0]
    return pl.pallas_call(
        functools.partial(pack_kernel, n_z, per, len(after)),
        out_shape=jax.ShapeDtypeStruct((n_dp, pairs, TILE, HEAD_DIM), pieces[0].dtype),
        in_specs=[SMEM] + [ANY] * (n_z + len(after)),
        out_specs=ANY,
        scratch_shapes=move_scratch(TILES, pairs, TILE, HEAD_DIM),
        compiler_params=pltpu.CompilerParams(vmem_limit_bytes=6 << 20),
        cost_estimate=copy_cost(pairs * ROW_TOK),
    )(tab, *pieces, *after)


def unpack_kernel(n_z, per, n_after, tab, got, *rest):
    pieces, scratch = rest[n_after : n_after + n_z], rest[-3:]
    moves = []
    for place, shift in enumerate(shift_order(n_z)):
        target = lax.rem(tab[ZPOS] + shift, n_z)
        for i in range(per):
            dest = tab[DEST + target * per + i]
            moves.append((got.at[dest], pieces[place].at[:, pl.ds(i * TILE, TILE), :]))
    run_moves(moves, *scratch)


def unpack_tiles(n_z, tab, got, after):
    per = TILES // n_z
    pairs = got.shape[1]
    piece = jax.ShapeDtypeStruct((pairs, per * TILE, HEAD_DIM), got.dtype)
    return pl.pallas_call(
        functools.partial(unpack_kernel, n_z, per, len(after)),
        out_shape=[piece] * n_z,
        in_specs=[SMEM, ANY] + [ANY] * len(after),
        out_specs=[ANY] * n_z,
        scratch_shapes=move_scratch(TILES, pairs, TILE, HEAD_DIM),
        compiler_params=pltpu.CompilerParams(vmem_limit_bytes=6 << 20),
        cost_estimate=copy_cost(pairs * ROW_TOK),
    )(tab, got, *after)


def join_kernel(unit, n_z, heads, n_prev, tab, *rest):
    pieces, outs, scratch = rest[:n_z], rest[n_z + n_prev : -3], rest[-3:]
    moves = []
    for place, shift in enumerate(shift_order(n_z)):
        group = lax.rem(tab[ZPOS] + n_z - shift, n_z)
        for i, (part, head) in enumerate(unit):
            col = pl.multiple_of((group * heads + head) * HEAD_DIM, HEAD_DIM)
            moves.append((pieces[place].at[i], outs[part].at[:, pl.ds(col, HEAD_DIM)]))
    run_moves(moves, *scratch)


def join_heads(unit, n_z, heads, tab, pieces, prev):
    rows = pieces[0].shape[1]
    out = jax.ShapeDtypeStruct((rows, n_z * heads * HEAD_DIM), pieces[0].dtype)
    return pl.pallas_call(
        functools.partial(join_kernel, unit, n_z, heads, len(prev)),
        out_shape=[out] * PARTS,
        in_specs=[SMEM] + [ANY] * (n_z + len(prev)),
        out_specs=[ANY] * PARTS,
        scratch_shapes=move_scratch(n_z * len(unit), rows, HEAD_DIM),
        input_output_aliases={1 + n_z + i: i for i in range(len(prev))},
        compiler_params=pltpu.CompilerParams(vmem_limit_bytes=6 << 20),
        cost_estimate=copy_cost(n_z * len(unit) * rows),
    )(tab, *pieces, *prev)


def attend_kernel(got_at, back_at, n_got, n_back, n_after, tab, grad, *rest):
    got, rest = rest[:n_got], rest[n_got + n_after :]
    att, back, rest = rest[0], rest[1 : 1 + n_back], rest[1 + n_back :]
    tiles, grads, in_sem, out_sem = rest
    scale = HEAD_DIM ** (-0.5)
    nt = (((1,), (1,)), ((), ()))
    tn = (((0,), (0,)), ((), ()))
    nn = (((1,), (0,)), ((), ()))

    def dot(a, b, dims):
        return lax.dot_general(a, b, dims, preferred_element_type=jnp.float32)

    run_copies(
        [
            pltpu.make_async_copy(
                got[u].at[tab[SOURCE + t], i],
                tiles.at[part, pl.ds(t * TILE, TILE), :],
                in_sem.at[t * PARTS + part],
            )
            for t in range(TILES)
            for part, (u, i) in enumerate(got_at)
        ]
    )

    def document(first, count):
        extent = count * TILE
        rows = pl.ds(pl.multiple_of(first * TILE, TILE), extent)
        q, k, v = tiles[0, rows, :], tiles[1, rows, :], tiles[2, rows, :]
        g = grad[rows, :]
        scores = dot(q, k, nt)
        later = lax.broadcasted_iota(jnp.int32, (extent, extent), 0)
        earlier = lax.broadcasted_iota(jnp.int32, (extent, extent), 1)
        scores = jnp.where(later >= earlier, scores, -jnp.inf)
        top = jnp.max(scores, axis=1, keepdims=True)
        weights = jnp.exp2((scores - top) * (scale * LOG2E))
        probs = weights * (1.0 / jnp.sum(weights, axis=1, keepdims=True))
        low = probs.astype(jnp.bfloat16)
        attended = dot(low, v, nn).astype(jnp.bfloat16)
        att[rows, :] = attended
        delta = jnp.sum(
            g.astype(jnp.float32) * attended.astype(jnp.float32), axis=1, keepdims=True
        )
        grads[2, rows, :] = dot(low, g, tn).astype(jnp.bfloat16)
        grad_scores = (probs * (dot(g, v, nt) - delta)).astype(jnp.bfloat16)
        grads[0, rows, :] = (dot(grad_scores, k, nn) * scale).astype(jnp.bfloat16)
        grads[1, rows, :] = (dot(grad_scores, q, tn) * scale).astype(jnp.bfloat16)

    def step(j, first):
        count = tab[DOCLEN + j]
        for size in range(1, DOC_MOST + 1):
            pl.when(count == size)(functools.partial(document, first, size))
        return first + count

    lax.fori_loop(0, DOCS, step, jnp.int32(0))
    run_copies(
        [
            pltpu.make_async_copy(
                grads.at[part, pl.ds(t * TILE, TILE), :],
                back[u].at[tab[SOURCE + t], i],
                out_sem.at[t * PARTS + part],
            )
            for t in range(TILES)
            for part, (u, i) in enumerate(back_at)
        ]
    )


def attend(head, tab, grad_out, got, got_at, back_pairs, back_at, prev, after):
    column = pl.BlockSpec((ROW_TOK, HEAD_DIM), lambda i: (0, head))
    slots = got[0].shape[0]
    n_got, n_after = len(got), len(after)
    return pl.pallas_call(
        functools.partial(
            attend_kernel, got_at, back_at, n_got, len(back_pairs), n_after + len(prev)
        ),
        grid=(1,),
        out_shape=[jax.ShapeDtypeStruct(grad_out.shape, grad_out.dtype)]
        + [
            jax.ShapeDtypeStruct((slots, pairs, TILE, HEAD_DIM), grad_out.dtype)
            for pairs in back_pairs
        ],
        in_specs=[SMEM, column] + [ANY] * (n_got + n_after + len(prev)),
        out_specs=[column] + [ANY] * len(back_pairs),
        scratch_shapes=[
            pltpu.VMEM((PARTS, ROW_TOK, HEAD_DIM), jnp.bfloat16),
            pltpu.VMEM((PARTS, ROW_TOK, HEAD_DIM), jnp.bfloat16),
            pltpu.SemaphoreType.DMA((TILES * PARTS,)),
            pltpu.SemaphoreType.DMA((TILES * PARTS,)),
        ],
        input_output_aliases={2 + n_got + n_after + i: i for i in range(len(prev))},
        compiler_params=pltpu.CompilerParams(vmem_limit_bytes=24 << 20),
        cost_estimate=pl.CostEstimate(
            flops=4 << 30, bytes_accessed=8 << 20, transcendentals=4 << 20
        ),
    )(tab, grad_out, *got, *after, *prev)


def shift_by(pieces, n_z):
    moved = []
    for piece, shift in zip(pieces, shift_order(n_z)):
        if shift:
            pairs = [(i, (i + shift) % n_z) for i in range(n_z)]
            piece = lax.ppermute(piece, "ulysses", pairs)
        moved.append(piece)
    return moved


def swap_rows(send):
    return lax.all_to_all(send, "dp", split_axis=0, concat_axis=0, tiled=True)


def shards(query_in, key_in, value_in, grad_out, packing, doc_tiles):
    n_dp = lax.axis_size("dp")
    n_z = lax.axis_size("ulysses")
    row_index = lax.axis_index("dp")
    heads = grad_out.shape[1] // HEAD_DIM
    dest = lax.dynamic_slice_in_dim(packing, row_index * TILES, TILES) // TILES
    place = row_index * TILES + jnp.arange(TILES, dtype=jnp.int32)
    source_row = jnp.arange(packing.shape[0], dtype=jnp.int32) // TILES
    source = jnp.sum(
        jnp.where(packing[None, :] == place[:, None], source_row[None, :], 0),
        axis=1,
        dtype=jnp.int32,
    )
    tab = jnp.concatenate(
        [dest, source, lax.axis_index("ulysses")[None].astype(jnp.int32), doc_tiles[0]]
    )

    whole = [[(part, head) for part in range(PARTS)] for head in range(heads)]
    ins = outs = whole

    def places(units, head):
        used = [u for u, unit in enumerate(units) if any(h == head for _, h in unit)]
        at = [
            next((i, units[u].index((part, head))) for i, u in enumerate(used) if (part, head) in units[u])
            for part in range(PARTS)
        ]
        return used, at

    pieces, after = [], ()
    for unit in ins:
        split = split_heads(unit, n_z, heads, tab, query_in, key_in, value_in, after)
        pieces.append(shift_by(split, n_z))
        after = (pieces[-1][1],)
    got, home, prev, moved = [], [], (), []

    def bring(u, after):
        if u + 1 < len(ins):
            after = after + (pieces[u + 1][0],)
        got.append(swap_rows(pack_tiles(n_dp, tab, pieces[u], after)))

    def attend_head(head, after):
        used, got_at = places(ins, head)
        targets, back_at = places(outs, head)
        attended, *sends = attend(
            head,
            tab,
            grad_out,
            [got[u] for u in used],
            got_at,
            [len(outs[u]) for u in targets],
            back_at,
            prev,
            after,
        )
        return attended, sends

    for head in range(heads):
        if head == 0:
            bring(0, ())
        attended, sends = attend_head(head, tuple(moved[0][1:]) if head == 1 else ())
        prev = (attended,)
        for send in sends:
            back = swap_rows(send)
            moved.append(shift_by(unpack_tiles(n_z, tab, back, ()), n_z))
        if head == 0:
            for u in range(1, len(ins)):
                bring(u, (sends[-1],) if u == 1 else (back,))

    grads = ()
    for unit, arrived in zip(outs, moved):
        grads = tuple(join_heads(unit, n_z, heads, tab, arrived, grads))
    return (attended,) + grads


def solution(mesh):
    in_specs = (
        P(("dp", "ulysses"), None),
        P(("dp", "ulysses"), None),
        P(("dp", "ulysses"), None),
        P("dp", "ulysses"),
        P(),
        P("dp", None),
    )
    out_specs = (
        P("dp", "ulysses"),
        P(("dp", "ulysses"), None),
        P(("dp", "ulysses"), None),
        P(("dp", "ulysses"), None),
    )
    return jax.shard_map(shards, mesh=mesh, in_specs=in_specs, out_specs=out_specs, check_vma=False)
```

```python
import functools
import jax
import jax.numpy as jnp
from jax import lax
from jax.experimental import pallas as pl
from jax.experimental.pallas import tpu as pltpu
from jax.sharding import PartitionSpec as P

HEAD_DIM = 128
TILE = 128
DOC_MOST = 4
ROW_TOK = 2048
TILES = 16
DOCS = 5
PARTS = 3
LOG2E = 1.4426950408889634
DEST, SOURCE, ZPOS, DOCLEN = 0, 16, 32, 33

ANY = pl.BlockSpec(memory_space=pl.ANY)
SMEM = pl.BlockSpec(memory_space=pltpu.SMEM)


def shift_order(n_z):
    order = [0]
    for step in range(n_z // 2 - 1, 0, -1):
        order += [step, n_z - step]
    return order[:3] + [n_z // 2] + order[3:]


def copy_cost(rows):
    return pl.CostEstimate(flops=0, bytes_accessed=4 * rows * HEAD_DIM, transcendentals=0)


def run_copies(copies):
    for copy in copies:
        copy.start()
    for copy in copies:
        copy.wait()


def run_moves(moves, held, in_sem, out_sem):
    loads, stores = [], []
    for i, (source, target) in enumerate(moves):
        loads.append(pltpu.make_async_copy(source, held.at[i], in_sem.at[i]))
        stores.append(pltpu.make_async_copy(held.at[i], target, out_sem.at[i]))
    for load in loads:
        load.start()
    for load, store in zip(loads, stores):
        load.wait()
        store.start()
    for store in stores:
        store.wait()


def move_scratch(count, *block):
    return [
        pltpu.VMEM((count,) + block, jnp.bfloat16),
        pltpu.SemaphoreType.DMA((count,)),
        pltpu.SemaphoreType.DMA((count,)),
    ]


def split_kernel(unit, n_z, heads, n_after, tab, q, k, v, *rest):
    outs, scratch = rest[n_after:-3], rest[-3:]
    moves = []
    for place, shift in enumerate(shift_order(n_z)):
        group = lax.rem(tab[ZPOS] + shift, n_z)
        for i, (part, head) in enumerate(unit):
            col = pl.multiple_of((group * heads + head) * HEAD_DIM, HEAD_DIM)
            moves.append(((q, k, v)[part].at[:, pl.ds(col, HEAD_DIM)], outs[place].at[i]))
    run_moves(moves, *scratch)


def split_heads(unit, n_z, heads, tab, q, k, v, after):
    rows = q.shape[0]
    return pl.pallas_call(
        functools.partial(split_kernel, unit, n_z, heads, len(after)),
        out_shape=[jax.ShapeDtypeStruct((len(unit), rows, HEAD_DIM), q.dtype)] * n_z,
        in_specs=[SMEM] + [ANY] * (3 + len(after)),
        out_specs=[ANY] * n_z,
        scratch_shapes=move_scratch(n_z * len(unit), rows, HEAD_DIM),
        compiler_params=pltpu.CompilerParams(vmem_limit_bytes=(6 if after else 60) << 20),
        cost_estimate=copy_cost(n_z * len(unit) * rows),
    )(tab, q, k, v, *after)


def pack_kernel(n_z, per, n_after, tab, *rest):
    pieces, send, scratch = rest[:n_z], rest[n_z + n_after], rest[-3:]
    moves = []
    for place, shift in enumerate(shift_order(n_z)):
        origin = lax.rem(tab[ZPOS] + n_z - shift, n_z)
        for i in range(per):
            dest = tab[DEST + origin * per + i]
            moves.append((pieces[place].at[:, pl.ds(i * TILE, TILE), :], send.at[dest]))
    run_moves(moves, *scratch)


def pack_tiles(n_dp, tab, pieces, after):
    n_z = len(pieces)
    per = TILES // n_z
    pairs = pieces[0].shape[0]
    return pl.pallas_call(
        functools.partial(pack_kernel, n_z, per, len(after)),
        out_shape=jax.ShapeDtypeStruct((n_dp, pairs, TILE, HEAD_DIM), pieces[0].dtype),
        in_specs=[SMEM] + [ANY] * (n_z + len(after)),
        out_specs=ANY,
        scratch_shapes=move_scratch(TILES, pairs, TILE, HEAD_DIM),
        compiler_params=pltpu.CompilerParams(vmem_limit_bytes=6 << 20),
        cost_estimate=copy_cost(pairs * ROW_TOK),
    )(tab, *pieces, *after)


def unpack_kernel(n_z, per, n_after, tab, got, *rest):
    pieces, scratch = rest[n_after : n_after + n_z], rest[-3:]
    moves = []
    for place, shift in enumerate(shift_order(n_z)):
        target = lax.rem(tab[ZPOS] + shift, n_z)
        for i in range(per):
            dest = tab[DEST + target * per + i]
            moves.append((got.at[dest], pieces[place].at[:, pl.ds(i * TILE, TILE), :]))
    run_moves(moves, *scratch)


def unpack_tiles(n_z, tab, got, after):
    per = TILES // n_z
    pairs = got.shape[1]
    piece = jax.ShapeDtypeStruct((pairs, per * TILE, HEAD_DIM), got.dtype)
    return pl.pallas_call(
        functools.partial(unpack_kernel, n_z, per, len(after)),
        out_shape=[piece] * n_z,
        in_specs=[SMEM, ANY] + [ANY] * len(after),
        out_specs=[ANY] * n_z,
        scratch_shapes=move_scratch(TILES, pairs, TILE, HEAD_DIM),
        compiler_params=pltpu.CompilerParams(vmem_limit_bytes=6 << 20),
        cost_estimate=copy_cost(pairs * ROW_TOK),
    )(tab, got, *after)


def join_kernel(unit, n_z, heads, n_prev, tab, *rest):
    pieces, outs, scratch = rest[:n_z], rest[n_z + n_prev : -3], rest[-3:]
    moves = []
    for place, shift in enumerate(shift_order(n_z)):
        group = lax.rem(tab[ZPOS] + n_z - shift, n_z)
        for i, (part, head) in enumerate(unit):
            col = pl.multiple_of((group * heads + head) * HEAD_DIM, HEAD_DIM)
            moves.append((pieces[place].at[i], outs[part].at[:, pl.ds(col, HEAD_DIM)]))
    run_moves(moves, *scratch)


def join_heads(unit, n_z, heads, tab, pieces, prev):
    rows = pieces[0].shape[1]
    out = jax.ShapeDtypeStruct((rows, n_z * heads * HEAD_DIM), pieces[0].dtype)
    return pl.pallas_call(
        functools.partial(join_kernel, unit, n_z, heads, len(prev)),
        out_shape=[out] * PARTS,
        in_specs=[SMEM] + [ANY] * (n_z + len(prev)),
        out_specs=[ANY] * PARTS,
        scratch_shapes=move_scratch(n_z * len(unit), rows, HEAD_DIM),
        input_output_aliases={1 + n_z + i: i for i in range(len(prev))},
        compiler_params=pltpu.CompilerParams(vmem_limit_bytes=6 << 20),
        cost_estimate=copy_cost(n_z * len(unit) * rows),
    )(tab, *pieces, *prev)


def attend_kernel(got_at, back_at, n_got, n_back, n_after, tab, grad, *rest):
    got, rest = rest[:n_got], rest[n_got + n_after :]
    att, back, rest = rest[0], rest[1 : 1 + n_back], rest[1 + n_back :]
    tiles, grads, in_sem, out_sem = rest
    scale = HEAD_DIM ** (-0.5)
    nt = (((1,), (1,)), ((), ()))
    tn = (((0,), (0,)), ((), ()))
    nn = (((1,), (0,)), ((), ()))

    def dot(a, b, dims):
        return lax.dot_general(a, b, dims, preferred_element_type=jnp.float32)

    run_copies(
        [
            pltpu.make_async_copy(
                got[u].at[tab[SOURCE + t], i],
                tiles.at[part, pl.ds(t * TILE, TILE), :],
                in_sem.at[t * PARTS + part],
            )
            for t in range(TILES)
            for part, (u, i) in enumerate(got_at)
        ]
    )

    def document(first, count):
        extent = count * TILE
        rows = pl.ds(pl.multiple_of(first * TILE, TILE), extent)
        q, k, v = tiles[0, rows, :], tiles[1, rows, :], tiles[2, rows, :]
        g = grad[rows, :]
        scores = dot(q, k, nt)
        later = lax.broadcasted_iota(jnp.int32, (extent, extent), 0)
        earlier = lax.broadcasted_iota(jnp.int32, (extent, extent), 1)
        scores = jnp.where(later >= earlier, scores, -jnp.inf)
        top = jnp.max(scores, axis=1, keepdims=True)
        weights = jnp.exp2((scores - top) * (scale * LOG2E))
        probs = weights * (1.0 / jnp.sum(weights, axis=1, keepdims=True))
        low = probs.astype(jnp.bfloat16)
        attended = dot(low, v, nn).astype(jnp.bfloat16)
        att[rows, :] = attended
        delta = jnp.sum(
            g.astype(jnp.float32) * attended.astype(jnp.float32), axis=1, keepdims=True
        )
        grads[2, rows, :] = dot(low, g, tn).astype(jnp.bfloat16)
        grad_scores = (probs * (dot(g, v, nt) - delta)).astype(jnp.bfloat16)
        grads[0, rows, :] = (dot(grad_scores, k, nn) * scale).astype(jnp.bfloat16)
        grads[1, rows, :] = (dot(grad_scores, q, tn) * scale).astype(jnp.bfloat16)

    def step(j, first):
        count = tab[DOCLEN + j]
        for size in range(1, DOC_MOST + 1):
            pl.when(count == size)(functools.partial(document, first, size))
        return first + count

    lax.fori_loop(0, DOCS, step, jnp.int32(0))
    run_copies(
        [
            pltpu.make_async_copy(
                grads.at[part, pl.ds(t * TILE, TILE), :],
                back[u].at[tab[SOURCE + t], i],
                out_sem.at[t * PARTS + part],
            )
            for t in range(TILES)
            for part, (u, i) in enumerate(back_at)
        ]
    )


def attend(head, tab, grad_out, got, got_at, back_pairs, back_at, prev, after):
    column = pl.BlockSpec((ROW_TOK, HEAD_DIM), lambda i: (0, head))
    slots = got[0].shape[0]
    n_got, n_after = len(got), len(after)
    return pl.pallas_call(
        functools.partial(
            attend_kernel, got_at, back_at, n_got, len(back_pairs), n_after + len(prev)
        ),
        grid=(1,),
        out_shape=[jax.ShapeDtypeStruct(grad_out.shape, grad_out.dtype)]
        + [
            jax.ShapeDtypeStruct((slots, pairs, TILE, HEAD_DIM), grad_out.dtype)
            for pairs in back_pairs
        ],
        in_specs=[SMEM, column] + [ANY] * (n_got + n_after + len(prev)),
        out_specs=[column] + [ANY] * len(back_pairs),
        scratch_shapes=[
            pltpu.VMEM((PARTS, ROW_TOK, HEAD_DIM), jnp.bfloat16),
            pltpu.VMEM((PARTS, ROW_TOK, HEAD_DIM), jnp.bfloat16),
            pltpu.SemaphoreType.DMA((TILES * PARTS,)),
            pltpu.SemaphoreType.DMA((TILES * PARTS,)),
        ],
        input_output_aliases={2 + n_got + n_after + i: i for i in range(len(prev))},
        compiler_params=pltpu.CompilerParams(vmem_limit_bytes=24 << 20),
        cost_estimate=pl.CostEstimate(
            flops=4 << 30, bytes_accessed=8 << 20, transcendentals=4 << 20
        ),
    )(tab, grad_out, *got, *after, *prev)


def shift_by(pieces, n_z):
    moved = []
    for piece, shift in zip(pieces, shift_order(n_z)):
        if shift:
            pairs = [(i, (i + shift) % n_z) for i in range(n_z)]
            piece = lax.ppermute(piece, "ulysses", pairs)
        moved.append(piece)
    return moved


def swap_rows(send):
    return lax.all_to_all(send, "dp", split_axis=0, concat_axis=0, tiled=True)


def shards(query_in, key_in, value_in, grad_out, packing, doc_tiles):
    n_dp = lax.axis_size("dp")
    n_z = lax.axis_size("ulysses")
    row_index = lax.axis_index("dp")
    heads = grad_out.shape[1] // HEAD_DIM
    dest = lax.dynamic_slice_in_dim(packing, row_index * TILES, TILES) // TILES
    place = row_index * TILES + jnp.arange(TILES, dtype=jnp.int32)
    source_row = jnp.arange(packing.shape[0], dtype=jnp.int32) // TILES
    source = jnp.sum(
        jnp.where(packing[None, :] == place[:, None], source_row[None, :], 0),
        axis=1,
        dtype=jnp.int32,
    )
    tab = jnp.concatenate(
        [dest, source, lax.axis_index("ulysses")[None].astype(jnp.int32), doc_tiles[0]]
    )

    whole = [[(part, head) for part in range(PARTS)] for head in range(heads)]
    ins = outs = whole

    def places(units, head):
        used = [u for u, unit in enumerate(units) if any(h == head for _, h in unit)]
        at = [
            next((i, units[u].index((part, head))) for i, u in enumerate(used) if (part, head) in units[u])
            for part in range(PARTS)
        ]
        return used, at

    pieces, after = [], ()
    for unit in ins:
        split = split_heads(unit, n_z, heads, tab, query_in, key_in, value_in, after)
        pieces.append(shift_by(split, n_z))
        after = (pieces[-1][1],)
    got, home, prev, moved = [], [], (), []

    def bring(u, after):
        if u + 1 < len(ins):
            after = after + (pieces[u + 1][0],)
        got.append(swap_rows(pack_tiles(n_dp, tab, pieces[u], after)))

    def attend_head(head, after):
        used, got_at = places(ins, head)
        targets, back_at = places(outs, head)
        attended, *sends = attend(
            head,
            tab,
            grad_out,
            [got[u] for u in used],
            got_at,
            [len(outs[u]) for u in targets],
            back_at,
            prev,
            after,
        )
        return attended, sends

    for head in range(heads):
        if head == 0:
            bring(0, ())
        after = ()
        if head == 0:
            after = tuple(pieces[1][1:5])
        elif head == 1:
            after = tuple(moved[0][1:])
        attended, sends = attend_head(head, after)
        prev = (attended,)
        for send in sends:
            back = swap_rows(send)
            after = tuple(moved[1][1:6]) if head == 2 else ()
            moved.append(shift_by(unpack_tiles(n_z, tab, back, after), n_z))
        if head == 0:
            bring(1, (sends[-1],) + tuple(pieces[2][1:5]))
            bring(2, (back,) + tuple(moved[0][1:5]))

    grads = ()
    for unit, arrived in zip(outs, moved):
        grads = tuple(join_heads(unit, n_z, heads, tab, arrived, grads))
    return (attended,) + grads


def solution(mesh):
    in_specs = (
        P(("dp", "ulysses"), None),
        P(("dp", "ulysses"), None),
        P(("dp", "ulysses"), None),
        P("dp", "ulysses"),
        P(),
        P("dp", None),
    )
    out_specs = (
        P("dp", "ulysses"),
        P(("dp", "ulysses"), None),
        P(("dp", "ulysses"), None),
        P(("dp", "ulysses"), None),
    )
    return jax.shard_map(shards, mesh=mesh, in_specs=in_specs, out_specs=out_specs, check_vma=False)
```
